256 devices in a mesh: loop: 8 (over x, core), rep: 32 (over z, y).
Axes of the slice: x: 4, y: 4, z: 8, core: 2. Of those that a mesh axis runs over, the one named last changes fastest.
Arguments:
- features: bfloat16 [65536, 512], P(('loop', 'rep')), may hold values from -6 to 6
- tiles: bfloat16 [20480, 128, 128], P(('loop', 'rep')), may hold values from -0.59765625 to 0.59765625
- slot_tile_row: int32 [20480], P(('loop', 'rep')), may hold values from 0 to 63
- slot_tile_column: int32 [20480], P(('loop', 'rep')), may hold values from 0 to 1
- counts: int32 [1280], P(('loop', 'rep')), may hold values from 1 to 16, as said below
- degree: int32 [65536], P(('loop', 'rep')), may hold values from 1 to 8
- w_self: bfloat16 [512, 512], replicated, may hold values from -0.25 to 0.25
- w_neigh: bfloat16 [512, 512], replicated, may hold values from -0.25 to 0.25
Outputs:
- updated: bfloat16 [65536, 512], P(('loop', 'rep'))
The draws below stay inside these ranges and needn't reach their ends.
Inputs may be any that keep to these rules, and one draw needn't show every extreme that they name: `counts`: each group has at least one live slot, and in every draw some group has all 16 slots live.
All inputs are finite; a program needn't handle non-finite values.
Results may differ from the reference program's by a relative error of at most 0.0045.
Values may be sent and summed in bfloat16 or wider, within the bound.
A program may use at most 128 MiB of HBM per device.

```python
import jax
import jax.numpy as jnp
from jax import lax

H = 512
TILE_WIDTH = 128
DEVICE_NODES = 256
CAP = 16
SPAN = 2
STEPS = 5
BLOCK_TILE_ROWS = 64
NODES = 65536
SLOT_COUNT = 20480
NCOUNT = 1280
N_LOOP = 8
N_REP = 32


def draw_counts(key, part):
    first, second, third = jax.random.split(jax.random.fold_in(key, 17), 3)
    upper = jax.random.randint(first, (NCOUNT,), 0, CAP + 1)
    lower = jax.random.randint(second, (NCOUNT,), 0, CAP + 1)
    values = jnp.minimum(1 + upper * lower // CAP, CAP)
    chosen = jax.random.randint(third, (), 0, NCOUNT)
    return jnp.where(jnp.arange(NCOUNT) == chosen, CAP, values).astype(jnp.int32)


def plant(result, rng, smallest, high):
    longest = result.shape.index(max(result.shape))
    spots = []
    for shift in (0, 1):
        where = [jax.random.randint(jax.random.fold_in(rng, axis), (), 0, length) for axis, length in enumerate(result.shape)]
        where[longest] = (where[longest] + shift) % result.shape[longest]
        spots.append(tuple(where))
    return result.at[spots[0]].set(smallest).at[spots[1]].set(high)


def shard_levels(key, extent, cuts, least, top_value):
    def one(position, blocks):
        heights = jax.random.uniform(jax.random.fold_in(jax.random.fold_in(key, 6), position), (blocks,), jnp.float32, least / len(cuts), top_value / len(cuts))
        return jnp.repeat(jnp.exp(heights), extent[position] // blocks).reshape((-1,) + (1,) * (len(extent) - position - 1))

    factor_of = one(*cuts[0])
    for cut in cuts[1:]:
        factor_of = factor_of * one(*cut)
    return factor_of


def gaussian(rng, dims, spread, bound, cuts=(), held_as=jnp.bfloat16):
    factor_of = shard_levels(rng, dims, cuts, -0.22, 0.18) if cuts else 1.0
    array = jax.random.normal(rng, dims, jnp.float32) * spread * factor_of
    return jnp.minimum(jnp.maximum(array, -bound), bound).astype(held_as)


def setup_inputs(seed: int = 0) -> dict:
    seeds = jax.random.split(jax.random.key(seed), 9)
    return {
        "features": gaussian(seeds[0], (NODES, H), 1.0, 6.0, ((0, 256),)),
        "tiles": gaussian(seeds[1], (SLOT_COUNT, TILE_WIDTH, TILE_WIDTH), 0.1, 0.59765625, ((0, 256),)),
        "slot_tile_row": plant(jax.random.randint(seeds[2], (SLOT_COUNT,), 0, BLOCK_TILE_ROWS), jax.random.fold_in(seeds[2], 1), 0, BLOCK_TILE_ROWS - 1).astype(jnp.int32),
        "slot_tile_column": plant(jax.random.randint(seeds[3], (SLOT_COUNT,), 0, DEVICE_NODES // TILE_WIDTH), jax.random.fold_in(seeds[3], 1), 0, (DEVICE_NODES // TILE_WIDTH) - 1).astype(jnp.int32),
        "counts": draw_counts(jax.random.fold_in(seeds[8], 71), 0),
        "degree": plant(jax.random.randint(seeds[5], (NODES,), 1, 9), jax.random.fold_in(seeds[5], 1), 1, 8).astype(jnp.int32),
        "w_self": gaussian(seeds[6], (H, H), H ** -0.5, 0.25),
        "w_neigh": gaussian(seeds[7], (H, H), H ** -0.5, 0.25),
    }


def reference(features, tiles, slot_tile_row, slot_tile_column, counts, degree, w_self, w_neigh):
    ncol = DEVICE_NODES // TILE_WIDTH
    node_row_blocks = DEVICE_NODES * N_REP // TILE_WIDTH
    feat = features.reshape(N_LOOP, N_REP, ncol, TILE_WIDTH, H)
    tile_all = tiles.reshape(N_LOOP, N_REP, STEPS, CAP, TILE_WIDTH, TILE_WIDTH)
    rows_all = slot_tile_row.reshape(N_LOOP, N_REP, STEPS, CAP)
    cols_all = slot_tile_column.reshape(N_LOOP, N_REP, STEPS, CAP)
    count_all = counts.reshape(N_LOOP, N_REP, STEPS)
    slot_ids = jnp.arange(CAP, dtype=jnp.int32)
    block_ids = jnp.arange(node_row_blocks, dtype=jnp.int32)

    def one_block(index):
        total = jnp.zeros((node_row_blocks, TILE_WIDTH, H), jnp.float32)
        for rep in range(N_REP):
            for step in range(STEPS):
                source_block = (index + step - SPAN) % N_LOOP
                source = feat[source_block, rep]
                picked = jnp.take(source, cols_all[index, rep, step], axis=0).astype(jnp.float32)
                weights = tile_all[index, rep, step].astype(jnp.float32)
                prod = jnp.einsum("cab,cbh->cah", weights, picked, precision=lax.Precision.HIGHEST)
                live = slot_ids < count_all[index, rep, step]
                indicator_matrix = ((rows_all[index, rep, step][None, :] == block_ids[:, None]) & live[None, :]).astype(jnp.float32)
                total = total + jnp.einsum("pc,cah->pah", indicator_matrix, prod, precision=lax.Precision.HIGHEST)
        return total

    summed = lax.map(one_block, jnp.arange(N_LOOP, dtype=jnp.int32)).reshape(NODES, H)
    mean = (summed / degree.astype(jnp.float32)[:, None]).astype(jnp.bfloat16)
    both = jnp.dot(features, w_self, preferred_element_type=jnp.float32) + jnp.dot(mean, w_neigh, preferred_element_type=jnp.float32)
    return jnp.maximum(both, 0.0).astype(jnp.bfloat16)
```

```python
import functools

import jax
import jax.numpy as jnp
from jax import lax
from jax.experimental import pallas as pl
from jax.experimental.pallas import tpu as pltpu
from jax.sharding import PartitionSpec as P

RING_Y = 4
WIDTH = 128
ROWS_A = 160
UNROLL = 4
MULTIPLY, HALO, OWN = -1, -2, -3
SCHEDULE = (
    (0, MULTIPLY), (0, 0), (2, HALO), (3, HALO), (1, MULTIPLY), (0, 1),
    (1, 0), (0, 2), (2, MULTIPLY), (0, 3), (1, 1),
    (2, 0), (0, 4), (1, 2), (3, MULTIPLY), (0, 5), (1, 3), (2, 1),
    (3, 0), (0, OWN), (0, 6), (1, 4), (2, 2), (1, 5), (2, 3), (3, 1),
    (1, 6), (2, 4), (3, 2), (2, 5), (3, 3), (2, 6), (3, 4), (3, 5), (3, 6),
)
F32 = jnp.float32
BF16 = jnp.bfloat16


class Ring:
    def __init__(self, n, peers, chunk, half, add, recv_half, recv_full, send_sem, recv_sem):
        self.n, self.last = n, n // 2
        self.peers, self.chunk, self.half, self.add = peers, chunk, half, add
        self.recv_half, self.recv_full = recv_half, recv_full
        self.send_sem, self.recv_sem = send_sem, recv_sem

    def offset(self, way, step):
        distance = self.last + 1 - step
        return distance if way == 0 else self.n - distance

    def slot(self, way, step):
        return self.recv_half.at[way] if step == 1 else self.recv_full.at[way, step - 2]

    def copy(self, way, step, part):
        source = self.chunk(self.offset(way, step))
        target = self.slot(way, step)
        which = way if part == 0 else 1 - way
        if part < 2:
            source = self.half(source, which)
        if part < 2 and step > 1:
            target = self.half(target, which)
        index = {(1, 0): 0, (2, 1): 1, (2, 0): 2}.get((step, part), step)
        return pltpu.make_async_remote_copy(
            src_ref=source,
            dst_ref=target,
            send_sem=self.send_sem.at[way, index],
            recv_sem=self.recv_sem.at[way, index],
            device_id={"rep": self.peers[way]},
            device_id_type=pl.DeviceIdType.MESH,
        )

    def parts(self, step):
        return {1: (0,), 2: (1, 0)}.get(step, (2,))

    def first(self):
        for way in (0, 1):
            self.copy(way, 1, 0).start()
        for way in (0, 1):
            self.copy(way, 2, 1).start()

    def forward(self, step):
        for way in (0, 1):
            for part in self.parts(step - 1):
                self.copy(way, step - 1, part).wait_recv()
            source = self.chunk(self.offset(way, step))
            arrived = self.slot(way, step - 1)
            if step == 2:
                source = self.half(source, way)
            self.add(source, arrived)
            self.copy(way, step, 0 if step == 2 else 2).start()

    def finish(self):
        for way in (0, 1):
            for part in self.parts(self.last):
                self.copy(way, self.last, part).wait_recv()
        return self.slot(0, self.last), self.slot(1, self.last)

    def drain(self):
        for way in (0, 1):
            for step in range(1, self.last + 1):
                for part in self.parts(step):
                    self.copy(way, step, part).wait_send()


def add_into(target, arrived):
    if len(target.shape) == 2:
        target[...] = target[...] + arrived[...]
    else:

        def one(i, carry):
            target[i] = target[i] + arrived[i]
            return carry

        lax.fori_loop(0, target.shape[0], one, 0)


def split_leading(ref, which):
    size = ref.shape[0] // 2
    return ref.at[pl.ds(which * size, size)]


def kernel(
    row, column, counts, features, tiles, degree, w_self, w_neigh, out,
    tiles_v, terms, partial, self_v, neigh_v, scale, acc, summed,
    ay_half, ay_full, az_half, az_full, bz_half, bz_full, by_half, by_full,
    ay_send, ay_recv, az_send, az_recv, bz_send, bz_recv, by_send, by_recv,
    halo_send, halo_recv, local_sem, found, links, *source,
):
    groups, ring_z, ring_y, rows, width = partial.shape
    slots, tile = tiles.shape[0], tiles.shape[1]
    steps = source[0].shape[0]
    span = steps // 2
    capacity = slots // steps
    n_loop = lax.axis_size("loop")
    me_loop = lax.axis_index("loop")
    me = lax.axis_index("rep")
    y, z = lax.rem(me, ring_y), lax.div(me, ring_y)

    def at(zz, yy):
        return lax.rem(zz, ring_z) * ring_y + lax.rem(yy, ring_y)

    y_peers = (at(z, y + 1), at(z, y + ring_y - 1))
    z_peers = (at(z + 1, y), at(z + ring_z - 1, y))
    hops = [d for d in range(-span, span + 1) if d != 0]
    loop_peers = {d: lax.rem(me_loop + d + n_loop, n_loop) for d in hops}

    tile_copy = pltpu.make_async_copy(tiles, tiles_v, local_sem.at[0])
    self_copy = pltpu.make_async_copy(w_self, self_v, local_sem.at[1])
    neigh_copy = pltpu.make_async_copy(w_neigh, neigh_v, local_sem.at[2])
    tile_copy.start()

    def columns(h):
        return features.at[:, :, pl.ds(h * width, width)]

    own = [pltpu.make_async_copy(columns(h), source[h].at[span], local_sem.at[3 + h]) for h in range(groups)]
    for copy in own:
        copy.start()
    self_copy.start()
    neigh_copy.start()

    barrier = pltpu.get_barrier_semaphore()
    for d in hops:
        pl.semaphore_signal(barrier, inc=1, device_id={"loop": loop_peers[d]}, device_id_type=pl.DeviceIdType.MESH)
    for peer in y_peers + z_peers:
        pl.semaphore_signal(barrier, inc=1, device_id={"rep": peer}, device_id_type=pl.DeviceIdType.MESH)
    pl.semaphore_wait(barrier, len(hops) + 4)

    def link_slots():
        shape = (tile, tile)
        slot = lax.broadcasted_iota(jnp.int32, shape, 0)
        lane = lax.broadcasted_iota(jnp.int32, shape, 1)
        found[...] = jnp.full(found.shape, -1, jnp.int32)
        found[pl.ds(0, 1), pl.ds(0, slots)] = row[...]
        across = jnp.broadcast_to(found[pl.ds(0, 1), :], shape)
        down = across.astype(F32).T.astype(jnp.int32)
        before = jnp.where((down == across) & (slot < lane), slot + 1, 0)
        ending = jnp.where(down == lane, slot + 1, 0)
        found[pl.ds(0, 1), :] = jnp.max(before, axis=0, keepdims=True)
        found[pl.ds(1, 1), :] = jnp.max(ending, axis=0, keepdims=True)

    link_copy = pltpu.make_async_copy(found, links, local_sem.at[3 + groups])

    halo = [
        [
            pltpu.make_async_remote_copy(
                src_ref=columns(h),
                dst_ref=source[h].at[span - d],
                send_sem=halo_send.at[h, span - d],
                recv_sem=halo_recv.at[h, span - d],
                device_id={"loop": loop_peers[d]},
                device_id_type=pl.DeviceIdType.MESH,
            )
            for d in hops
        ]
        for h in range(groups)
    ]

    def start_halo(h):
        for copy in halo[h]:
            copy.start()

    def multiply(h):
        own[h].wait()
        for copy in halo[h]:
            copy.wait_recv()

        def some(i, carry):
            products = []
            for u in range(UNROLL):
                s = i * UNROLL + u
                k = lax.div(s, capacity)
                product = jnp.dot(tiles_v[s], source[h][k, column[s]], preferred_element_type=F32)
                products.append(product)
            for u in range(UNROLL):
                s = i * UNROLL + u
                k = lax.div(s, capacity)
                live = jnp.where(s - k * capacity < counts[k], 1.0, 0.0)
                terms[s + 1] = products[u] * live + terms[links[0, s]]
            return carry

        lax.fori_loop(0, slots // UNROLL, some, 0)

        def place(d, carry):
            for t in range(rows // tile):
                term = terms[links[1, d * (rows // tile) + t]]
                partial[h, lax.div(d, ring_y), lax.rem(d, ring_y), pl.ds(t * tile, tile)] = term.astype(BF16)
            return carry

        lax.fori_loop(0, ring_z * ring_y, place, 0)

    def rings(h):
        part = partial.at[h]
        rows_b = rows - ROWS_A
        lane_a = part.at[z, y, pl.ds(0, ROWS_A)]
        lane_b = part.at[z, y, pl.ds(ROWS_A, rows_b)]
        ay = Ring(
            ring_y, y_peers, lambda o: part.at[:, lax.rem(y + o, ring_y), pl.ds(0, ROWS_A)], split_leading, add_into,
            ay_half.at[h], ay_full.at[h], ay_send.at[h], ay_recv.at[h],
        )
        az = Ring(
            ring_z, z_peers, lambda o: part.at[lax.rem(z + o, ring_z), y, pl.ds(0, ROWS_A)], split_leading, add_into,
            az_half.at[h], az_full.at[h], az_send.at[h], az_recv.at[h],
        )
        bz = Ring(
            ring_z, z_peers, lambda o: part.at[lax.rem(z + o, ring_z), :, pl.ds(ROWS_A, rows_b)], split_leading, add_into,
            bz_half.at[h], bz_full.at[h], bz_send.at[h], bz_recv.at[h],
        )
        by = Ring(
            ring_y, y_peers, lambda o: part.at[z, lax.rem(y + o, ring_y), pl.ds(ROWS_A, rows_b)], split_leading, add_into,
            by_half.at[h], by_full.at[h], by_send.at[h], by_recv.at[h],
        )
        return ay, az, bz, by, lane_a, lane_b

    made = [rings(h) for h in range(groups)]

    def join(target, pair):
        left, right = pair

        def one(i, carry):
            total = target[i].astype(F32) + left[i].astype(F32) + right[i].astype(F32)
            target[i] = total.astype(BF16)
            return carry

        lax.fori_loop(0, target.shape[0], one, 0)

    def phase(h, p):
        ay, az, bz, by, lane_a, lane_b = made[h]
        if p == 0:
            ay.first()
            bz.first()
        elif p == 1:
            ay.forward(2)
            bz.forward(2)
        elif p == 2:
            join(partial.at[h, :, y, pl.ds(0, ROWS_A)], ay.finish())
            az.first()
            bz.forward(3)
        elif p == 3:
            az.forward(2)
            bz.forward(4)
        elif p == 4:
            join(partial.at[h, z, :, pl.ds(ROWS_A, rows - ROWS_A)], bz.finish())
            by.first()
            az.forward(3)
        elif p == 5:
            az.forward(4)
            by.forward(2)
        elif p == 6:
            left, right = az.finish()
            summed[pl.ds(0, ROWS_A)] = lane_a[...].astype(F32) + left[...].astype(F32) + right[...].astype(F32)
            left, right = by.finish()
            summed[pl.ds(ROWS_A, rows - ROWS_A)] = lane_b[...].astype(F32) + left[...].astype(F32) + right[...].astype(F32)
            mean = (summed[...] / scale[...]).astype(BF16)
            acc[...] += jnp.dot(mean, neigh_v[pl.ds(h * width, width)], preferred_element_type=F32)

    start_halo(0)
    start_halo(1)
    link_slots()
    link_copy.start()
    terms[0] = jnp.zeros_like(terms[0])
    for t in range(rows // tile):
        line = jnp.broadcast_to(degree[pl.ds(t, 1), :].astype(F32), (tile, tile))
        scale[pl.ds(t * tile, tile)] = line.T
    link_copy.wait()
    tile_copy.wait()
    for h, p in SCHEDULE:
        if p == MULTIPLY:
            multiply(h)
        elif p == HALO:
            start_halo(h)
        elif p == OWN:
            self_copy.wait()
            neigh_copy.wait()
            total = jnp.zeros(acc.shape, F32)
            for g in range(groups):
                mine = source[g][span].reshape(rows, width)
                total += jnp.dot(mine, self_v[pl.ds(g * width, width)], preferred_element_type=F32)
            acc[...] = total
        else:
            phase(h, p)
    out[...] = jnp.maximum(acc[...], 0.0).astype(out.dtype)

    for h in range(groups):
        for copy in halo[h]:
            copy.wait_send()
        for ring in made[h][:4]:
            ring.drain()


def shards(features, tiles, slot_tile_row, slot_tile_column, counts, degree, w_self, w_neigh):
    rows, hidden = features.shape
    slots, tile = tiles.shape[0], tiles.shape[1]
    steps = counts.shape[0]
    ring_y = RING_Y
    ring_z = lax.axis_size("rep") // ring_y
    groups = hidden // WIDTH
    rows_b = rows - ROWS_A
    dma = pltpu.SemaphoreType.DMA

    def slots_of(n, chunk):
        half = (chunk[0] // 2,) + chunk[1:]
        return [
            pltpu.VMEM((groups, 2) + half + (WIDTH,), BF16),
            pltpu.VMEM((groups, 2, n // 2 - 1) + chunk + (WIDTH,), BF16),
        ]

    smem = pl.BlockSpec(memory_space=pltpu.SMEM)
    vmem = pl.BlockSpec(memory_space=pltpu.VMEM)
    anywhere = pl.BlockSpec(memory_space=pl.ANY)
    n_y, n_z = ring_y // 2 + 1, ring_z // 2 + 1
    return pl.pallas_call(
        kernel,
        out_shape=jax.ShapeDtypeStruct((rows, hidden), BF16),
        in_specs=[vmem, smem, smem, anywhere, anywhere, vmem, anywhere, anywhere],
        out_specs=vmem,
        scratch_shapes=[
            pltpu.VMEM((slots, tile, tile), BF16),
            pltpu.VMEM((slots + 1, tile, WIDTH), F32),
            pltpu.VMEM((groups, ring_z, ring_y, rows, WIDTH), BF16),
            pltpu.VMEM(w_self.shape, BF16),
            pltpu.VMEM(w_neigh.shape, BF16),
            pltpu.VMEM((rows, WIDTH), F32),
            pltpu.VMEM((rows, hidden), F32),
            pltpu.VMEM((rows, WIDTH), F32),
            *slots_of(ring_y, (ring_z, ROWS_A)),
            *slots_of(ring_z, (ROWS_A,)),
            *slots_of(ring_z, (ring_y, rows_b)),
            *slots_of(ring_y, (rows_b,)),
            *[dma((groups, 2, n_y))] * 2,
            *[dma((groups, 2, n_z))] * 2,
            *[dma((groups, 2, n_z))] * 2,
            *[dma((groups, 2, n_y))] * 2,
            dma((groups, steps)),
            dma((groups, steps)),
            dma((4 + groups,)),
            pltpu.VMEM((8, tile), jnp.int32),
            pltpu.SMEM((8, tile), jnp.int32),
            *[pltpu.VMEM((steps, rows // tile, tile, WIDTH), BF16)] * groups,
        ],
        compiler_params=pltpu.CompilerParams(
            collective_id=0, has_side_effects=True, vmem_limit_bytes=56 * 1024 * 1024
        ),
    )(
        slot_tile_row.reshape(1, slots),
        slot_tile_column,
        counts,
        features.reshape(rows // tile, tile, hidden),
        tiles,
        degree.reshape(rows // tile, tile),
        w_self,
        w_neigh,
    )


def solution(mesh):
    return jax.shard_map(
        shards,
        mesh=mesh,
        in_specs=(
            P(("loop", "rep"), None),
            P(("loop", "rep"), None, None),
            P(("loop", "rep")),
            P(("loop", "rep")),
            P(("loop", "rep")),
            P(("loop", "rep")),
            P(),
            P(),
        ),
        out_specs=P(("loop", "rep"), None),
        check_vma=False,
    )
```

```python
import functools

import jax
import jax.numpy as jnp
from jax import lax
from jax.experimental import pallas as pl
from jax.experimental.pallas import tpu as pltpu
from jax.sharding import PartitionSpec as P

RING_Y = 4
WIDTH = 128
ROWS_A = 160
UNROLL = 4
SCHEDULE = (
    (0, "M", 0, 0), (0, "A", 1, 1), (0, "B", 1, 1), (0, "A", 2, 1), (0, "B", 2, 1), (0, "A", 4, 1), (0, "B", 0, 1),
    (0, "A", 0, 1), (0, "A", 3, 1), (2, "M", 0, 0), (2, "B", 1, 1), (2, "A", 1, 1), (2, "B", 2, 1), (2, "A", 2, 1),
    (0, "A", 1, 2), (0, "B", 1, 2), (0, "B", 0, 2), (1, "M", 0, 0), (1, "A", 3, 1), (1, "B", 1, 1), (1, "B", 0, 1),
    (1, "A", 0, 1), (1, "A", 2, 1), (1, "A", 1, 1), (1, "B", 2, 1), (2, "B", 1, 2), (2, "B", 0, 1), (0, "A", 0, 2),
    (0, "B", 2, 2), (2, "A", 0, 1), (0, "B", 1, 3), (3, "M", 0, 0), (3, "A", 0, 1), (3, "B", 0, 1), (3, "A", 1, 1),
    (3, "A", 2, 1), (3, "B", 1, 1), (3, "B", 2, 1), (1, "A", 2, 2), (2, "B", 0, 2), (1, "B", 1, 2), (1, "A", 0, 2),
    (1, "B", 2, 2), (1, "A", 3, 2), (0, "Z", 0, 1), (3, "B", 1, 2), (0, "A", 2, 2), (1, "B", 0, 2), (2, "A", 2, 2),
    (2, "A", 0, 2), (2, "B", 2, 2), (1, "B", 1, 3), (3, "A", 4, 1), (0, "B", 2, 3), (0, "B", 0, 3), (0, "A", 3, 2),
    (1, "Z", 0, 1), (1, "A", 1, 2), (2, "A", 3, 1), (2, "B", 0, 3), (3, "B", 2, 2), (1, "B", 0, 3), (3, "A", 0, 2),
    (3, "B", 0, 2), (3, "B", 1, 3), (1, "B", 2, 3), (2, "A", 4, 1), (2, "A", 1, 2), (2, "B", 0, 4), (3, "B", 2, 3),
    (0, "B", 2, 4), (2, "B", 2, 3), (1, "B", 0, 4), (3, "B", 0, 3), (0, "Z", 0, 2), (2, "Z", 0, 1), (3, "A", 1, 2),
    (2, "B", 1, 3), (1, "B", 1, 4), (1, "Y", 0, 1), (1, "Z", 0, 2), (1, "A", 4, 1), (3, "A", 2, 2), (0, "B", 0, 4),
    (3, "A", 4, 2), (2, "Y", 0, 1), (0, "B", 1, 4), (3, "B", 0, 4), (3, "B", 1, 4), (2, "Z", 0, 2), (0, "A", 4, 2),
    (3, "A", 3, 1), (3, "Z", 0, 1), (0, "Y", 0, 1), (0, "Z", 0, 3), (1, "B", 2, 4), (2, "A", 4, 2), (2, "B", 2, 4),
    (2, "B", 1, 4), (3, "Z", 0, 2), (2, "A", 3, 2), (1, "Z", 0, 3), (3, "Y", 0, 1), (2, "Z", 0, 3), (0, "Z", 0, 4),
    (3, "A", 3, 2), (2, "Y", 0, 2), (0, "Y", 0, 2), (1, "Y", 0, 2), (3, "Z", 0, 3), (1, "A", 4, 2), (3, "B", 2, 4),
    (1, "Z", 0, 4), (2, "Z", 0, 4), (3, "Y", 0, 2), (3, "Z", 0, 4), (0, "W", 0, 0), (0, "F", 0, 0), (1, "F", 0, 0),
    (2, "F", 0, 0), (3, "F", 0, 0),
)
F32 = jnp.float32
BF16 = jnp.bfloat16


class Ring:
    def __init__(self, n, peers, chunk, half, recv_half, recv_full, send_sem, recv_sem):
        self.n, self.last, self.peers, self.chunk, self.half = n, n // 2, peers, chunk, half
        self.recv_half, self.recv_full, self.send_sem, self.recv_sem = recv_half, recv_full, send_sem, recv_sem

    def offset(self, way, step):
        distance = self.last + 1 - step
        return distance if way == 0 else self.n - distance

    def slot(self, way, step):
        if step > 1:
            return self.recv_full(way, step - 2)
        return self.recv_half(way).at[pl.ds(0, self.source(way, 1).shape[0])]

    def source(self, way, step):
        source = self.chunk(self.offset(way, step))
        return self.half(source, way) if step == 1 else source

    def target(self, way, step):
        source = self.chunk(self.offset(way, step))
        return self.half(source, way) if step == 2 else source

    def copy(self, way, step):
        return pltpu.make_async_remote_copy(
            src_ref=self.source(way, step),
            dst_ref=self.slot(way, step),
            send_sem=self.send_sem.at[way, step - 1],
            recv_sem=self.recv_sem.at[way, step - 1],
            device_id={"rep": self.peers[way]},
            device_id_type=pl.DeviceIdType.MESH,
        )

    def send(self, way, step):
        self.copy(way, step).start()

    def arrived(self, way, step):
        self.copy(way, step).wait_recv()
        return self.slot(way, step)

    def drain(self):
        for way in (0, 1):
            for step in range(1, self.last + 1):
                self.copy(way, step).wait_send()


def halve(ref, which):
    size = ref.shape[0]
    first = size // 2 if size < 16 else (size // 16 + 1) // 2 * 16
    return ref.at[pl.ds(0, first)] if which == 0 else ref.at[pl.ds(first, size - first)]


def near_last(n):
    order = [n // 2]
    for distance in range(n // 2 - 1, 0, -1):
        order += [distance, n - distance]
    return order + [0]


def kernel(
    row_in, column_in, counts_in, features, tiles, degree_in, w_self, w_neigh, out,
    tiles_v, terms, partial, self_v, neigh_v, scale, acc, summed,
    ay_half, ay_full, az_half, az_full, bz_half, bz_full, by_half, by_full,
    ay_send, ay_recv, az_send, az_recv, bz_send, bz_recv, by_send, by_recv,
    halo_send, halo_recv, local_sem, found, links, row, column, counts, degree, *blocks,
):
    groups, ring_z, ring_y, rows, width = partial.shape
    mine, source = blocks[:groups], blocks[groups:]
    slots, tile = tiles.shape[0], tiles.shape[1]
    steps = source[0].shape[0]
    span = steps // 2
    capacity = slots // steps
    n_loop = lax.axis_size("loop")
    me_loop = lax.axis_index("loop")
    me = lax.axis_index("rep")
    y, z = lax.rem(me, ring_y), lax.div(me, ring_y)

    def at(zz, yy):
        return lax.rem(zz, ring_z) * ring_y + lax.rem(yy, ring_y)

    y_peers = (at(z, y + 1), at(z, y + ring_y - 1))
    z_peers = (at(z + 1, y), at(z + ring_z - 1, y))
    hops = [d for d in range(-span, span + 1) if d != 0]
    loop_peers = {d: lax.rem(me_loop + d + n_loop, n_loop) for d in hops}

    def columns(h):
        return features.at[:, :, pl.ds(h * width, width)]

    own = [pltpu.make_async_copy(columns(h), mine[h], local_sem.at[h]) for h in range(groups)]
    moves = ((row_in, row), (degree_in, degree), (column_in, column), (counts_in, counts), (found, links), (tiles, tiles_v), (w_self, self_v), (w_neigh, neigh_v))
    row_copy, degree_copy, column_copy, counts_copy, link_copy, tile_copy, self_copy, neigh_copy = (
        pltpu.make_async_copy(src, dst, local_sem.at[groups + n]) for n, (src, dst) in enumerate(moves)
    )
    row_copy.start()
    own[0].start()

    barrier = pltpu.get_barrier_semaphore()
    for d in hops:
        pl.semaphore_signal(barrier, inc=1, device_id={"loop": loop_peers[d]}, device_id_type=pl.DeviceIdType.MESH)
    for peer in y_peers + z_peers:
        pl.semaphore_signal(barrier, inc=1, device_id={"rep": peer}, device_id_type=pl.DeviceIdType.MESH)
    for copy in (degree_copy, column_copy, counts_copy, tile_copy, *own[1:], self_copy, neigh_copy):
        copy.start()

    def step_at(place):
        return span if place == 0 else place - 1 if place <= span else place

    def link_slots():
        shape = (tile, tile)
        slot = lax.broadcasted_iota(jnp.int32, shape, 0)
        lane = lax.broadcasted_iota(jnp.int32, shape, 1)
        found[...] = jnp.full(found.shape, -1, jnp.int32)
        for place in range(steps):
            found[pl.ds(0, 1), pl.ds(place * capacity, capacity)] = row[:, pl.ds(step_at(place) * capacity, capacity)]
        across = jnp.broadcast_to(found[pl.ds(0, 1), :], shape)
        down = across.astype(F32).T.astype(jnp.int32)
        before = jnp.where((down == across) & (slot < lane), slot + 1, 0)
        ending = jnp.where(down == lane, slot + 1, 0)
        found[pl.ds(0, 1), :] = jnp.max(before, axis=0, keepdims=True)
        found[pl.ds(1, 1), :] = jnp.max(ending, axis=0, keepdims=True)

    halo = [
        [
            pltpu.make_async_remote_copy(
                src_ref=mine[h],
                dst_ref=source[h].at[span - d],
                send_sem=halo_send.at[h, span - d],
                recv_sem=halo_recv.at[h, span - d],
                device_id={"loop": loop_peers[d]},
                device_id_type=pl.DeviceIdType.MESH,
            )
            for d in hops
        ]
        for h in range(groups)
    ]

    def start_halo(h):
        own[h].wait()
        for copy in halo[h]:
            copy.start()

    def multiply(h):
        def some(block, i, carry):
            where = lax.div(i * UNROLL, capacity)
            k = jnp.where(where == 0, span, jnp.where(where <= span, where - 1, where))
            first = i * UNROLL - where * capacity
            products = []
            for u in range(UNROLL):
                s = k * capacity + first + u
                products.append(jnp.dot(tiles_v[s], block(k, column[s]), preferred_element_type=F32))
            for u in range(UNROLL):
                s = i * UNROLL + u
                live = jnp.where(first + u < counts[k], 1.0, 0.0)
                terms[s + 1] = products[u] * live + terms[links[0, s]]
            return carry

        lax.fori_loop(0, capacity // UNROLL, functools.partial(some, lambda k, c: mine[h][c]), 0)
        for copy in halo[h]:
            copy.wait_recv()
        lax.fori_loop(capacity // UNROLL, slots // UNROLL, functools.partial(some, lambda k, c: source[h][k, c]), 0)

        def place(i, carry):
            zz, yy = lax.div(i, ring_y), lax.rem(i, ring_y)
            d = at(z + spot(zz, ring_z), y + spot(yy, ring_y))
            for t in range(rows // tile):
                term = terms[links[1, d * (rows // tile) + t]]
                partial[h, zz, yy, pl.ds(t * tile, tile)] = term.astype(BF16)
            return carry

        lax.fori_loop(0, ring_z * ring_y, place, 0)

    def spot(i, n):
        distance = n // 2 - lax.div(i + 1, 2)
        return jnp.where(lax.rem(i, 2) == 1, distance, n - distance)

    order_z, order_y = near_last(ring_z), near_last(ring_y)
    sets_z = [(0, 1)] + [(2 * q - 1, 2) for q in range(1, ring_z // 2)] + [(ring_z - 1, 1)]
    sets_y = [(0, 1)] + [(2 * q - 1, 2) for q in range(1, ring_y // 2)] + [(ring_y - 1, 1)]
    rows_b = rows - ROWS_A
    in_a, in_b = pl.ds(0, ROWS_A), pl.ds(ROWS_A, rows_b)

    def rings(h):
        part = partial.at[h]

        def unit_a(q):
            first, count = sets_z[q]

            def chunk(o):
                yy = order_y.index(o)
                return part.at[pl.ds(first, 2), yy, in_a] if count == 2 else part.at[first, yy, in_a]

            def half(way):
                return ay_half.at[h, way, pl.ds(q, 1)] if count == 2 else ay_half.at[h, way, q]

            def full(way, step):
                return ay_full.at[h, way, pl.ds(first, 2)] if count == 2 else ay_full.at[h, way, first]

            return Ring(ring_y, y_peers, chunk, halve, half, full, ay_send.at[h, q], ay_recv.at[h, q])

        def unit_b(q):
            first, count = sets_y[q]

            def chunk(o):
                zz = order_z.index(o)
                return part.at[zz, pl.ds(first, 2), in_b] if count == 2 else part.at[zz, first, in_b]

            def half(way):
                return bz_half.at[h, way, pl.ds(q, 1)] if count == 2 else bz_half.at[h, way, q]

            def full(way, step):
                return bz_full.at[h, way, step, pl.ds(first, 2)] if count == 2 else bz_full.at[h, way, step, first]

            return Ring(ring_z, z_peers, chunk, halve, half, full, bz_send.at[h, q], bz_recv.at[h, q])

        az = Ring(
            ring_z, z_peers, lambda o: part.at[order_z.index(o), ring_y - 1, in_a], halve,
            lambda way: az_half.at[h, way], lambda way, step: az_full.at[h, way, step], az_send.at[h], az_recv.at[h],
        )
        by = Ring(
            ring_y, y_peers, lambda o: part.at[ring_z - 1, order_y.index(o), in_b], halve,
            lambda way: by_half.at[h, way], lambda way, step: by_full.at[h, way, step], by_send.at[h], by_recv.at[h],
        )
        return [unit_a(q) for q in range(len(sets_z))], [unit_b(q) for q in range(len(sets_y))], az, by

    made = [rings(h) for h in range(groups)]

    def forward(ring, step):
        for way in (0, 1):
            if step > 1:
                arrived = ring.arrived(way, step - 1)
                target = ring.target(way, step)
                target[...] = target[...] + arrived[...]
            ring.send(way, step)

    def second(ring, unit, step):
        sides = [unit.arrived(way, unit.last) for way in (0, 1)]
        for way in (0, 1):
            target = ring.chunk(ring.offset(way, step))
            if step == 1 and way == 1:
                ring.send(way, step)
                continue
            total = target[...].astype(F32)
            for side in sides:
                total += (side[way] if len(side.shape) == 3 else side[...]).astype(F32)
            if step > 1:
                arrived = ring.arrived(way, step - 1)
                if step == 2:
                    place = ring.target(way, 2)
                    target[...] = total.astype(BF16)
                    size = place.shape[0]
                    half = total[:size] if way == 0 else total[target.shape[0] - size :]
                    place[...] = (half + arrived[...].astype(F32)).astype(BF16)
                else:
                    target[...] = (total + arrived[...].astype(F32)).astype(BF16)
            else:
                target[...] = total.astype(BF16)
            ring.send(way, step)

    def last(ring, unit, rows_of):
        total = ring.chunk(0)[...].astype(F32)
        for way in (0, 1):
            total += unit.arrived(way, unit.last)[...].astype(F32)
        for way in (0, 1):
            total += ring.arrived(way, ring.last)[...].astype(F32)
        summed[rows_of] = total

    def run(h, name, q, step):
        units_a, units_b, az, by = made[h]
        if name == "A":
            forward(units_a[q], step)
        elif name == "B":
            forward(units_b[q], step)
        elif name == "Z":
            second(az, units_a[step - 1], step)
        elif name == "Y":
            second(by, units_b[step - 1], step)
        elif name == "M":
            multiply(h)
        elif name == "W":
            self_copy.wait()
            neigh_copy.wait()
            total = jnp.zeros(acc.shape, F32)
            for g in range(groups):
                total += jnp.dot(mine[g][...].reshape(rows, width), self_v[pl.ds(g * width, width)], preferred_element_type=F32)
            acc[...] = total
        elif name == "F":
            last(az, units_a[-1], in_a)
            last(by, units_b[-1], in_b)
            mean = (summed[...] / scale[...]).astype(BF16)
            acc[...] += jnp.dot(mean, neigh_v[pl.ds(h * width, width)], preferred_element_type=F32)

    row_copy.wait()
    link_slots()
    link_copy.start()
    terms[0] = jnp.zeros_like(terms[0])
    pl.semaphore_wait(barrier, len(hops) + 4)
    for h in range(groups):
        start_halo(h)
    degree_copy.wait()
    for t in range(rows // tile):
        line = jnp.broadcast_to(degree[pl.ds(t, 1), :].astype(F32), (tile, tile))
        scale[pl.ds(t * tile, tile)] = line.T
    for copy in (link_copy, column_copy, counts_copy, tile_copy):
        copy.wait()
    for item in SCHEDULE:
        run(*item)
    out[...] = jnp.maximum(acc[...], 0.0).astype(out.dtype)

    for h in range(groups):
        for copy in halo[h]:
            copy.wait_send()
        units_a, units_b, az, by = made[h]
        for ring in (*units_a, *units_b, az, by):
            ring.drain()


def shards(features, tiles, slot_tile_row, slot_tile_column, counts, degree, w_self, w_neigh):
    rows, hidden = features.shape
    slots, tile = tiles.shape[0], tiles.shape[1]
    steps = counts.shape[0]
    ring_y = RING_Y
    ring_z = lax.axis_size("rep") // ring_y
    groups = hidden // WIDTH
    rows_b = rows - ROWS_A
    dma = pltpu.SemaphoreType.DMA

    def buffer(*shape):
        return pltpu.VMEM((groups, 2, *shape, WIDTH), BF16)

    n_a, n_b = ring_z // 2 + 1, ring_y // 2 + 1
    last_y, last_z = ring_y // 2, ring_z // 2
    vmem = pl.BlockSpec(memory_space=pltpu.VMEM)
    anywhere = pl.BlockSpec(memory_space=pl.ANY)
    return pl.pallas_call(
        kernel,
        out_shape=jax.ShapeDtypeStruct((rows, hidden), BF16),
        in_specs=[anywhere] * 8,
        out_specs=vmem,
        scratch_shapes=[
            pltpu.VMEM((slots, tile, tile), BF16),
            pltpu.VMEM((slots + 1, tile, WIDTH), F32),
            pltpu.VMEM((groups, ring_z, ring_y, rows, WIDTH), BF16),
            pltpu.VMEM(w_self.shape, BF16),
            pltpu.VMEM(w_neigh.shape, BF16),
            pltpu.VMEM((rows, WIDTH), F32),
            pltpu.VMEM((rows, hidden), F32),
            pltpu.VMEM((rows, WIDTH), F32),
            buffer(n_a, ROWS_A),
            buffer(ring_z, ROWS_A),
            buffer(ROWS_A),
            buffer(last_z - 1, ROWS_A),
            buffer(n_b, rows_b),
            buffer(last_z - 1, ring_y, rows_b),
            buffer(rows_b),
            buffer(last_y - 1, rows_b),
            *[dma((groups, n_a, 2, last_y))] * 2,
            *[dma((groups, 2, last_z))] * 2,
            *[dma((groups, n_b, 2, last_z))] * 2,
            *[dma((groups, 2, last_y))] * 2,
            dma((groups, steps)),
            dma((groups, steps)),
            dma((8 + groups,)),
            pltpu.VMEM((8, tile), jnp.int32),
            pltpu.SMEM((8, tile), jnp.int32),
            pltpu.VMEM((1, slots), jnp.int32),
            pltpu.SMEM((slots,), jnp.int32),
            pltpu.SMEM((steps,), jnp.int32),
            pltpu.VMEM((rows // tile, tile), jnp.int32),
            *[pltpu.VMEM((rows // tile, tile, WIDTH), BF16)] * groups,
            *[pltpu.VMEM((steps, rows // tile, tile, WIDTH), BF16)] * groups,
        ],
        compiler_params=pltpu.CompilerParams(
            collective_id=0, has_side_effects=True, vmem_limit_bytes=56 * 1024 * 1024
        ),
    )(
        slot_tile_row.reshape(1, slots),
        slot_tile_column,
        counts,
        features.reshape(rows // tile, tile, hidden),
        tiles,
        degree.reshape(rows // tile, tile),
        w_self,
        w_neigh,
    )


def solution(mesh):
    return jax.shard_map(
        shards,
        mesh=mesh,
        in_specs=(
            P(("loop", "rep"), None),
            P(("loop", "rep"), None, None),
            P(("loop", "rep")),
            P(("loop", "rep")),
            P(("loop", "rep")),
            P(("loop", "rep")),
            P(),
            P(),
        ),
        out_specs=P(("loop", "rep"), None),
        check_vma=False,
    )
```

```python
import functools

import jax
import jax.numpy as jnp
from jax import lax
from jax.experimental import pallas as pl
from jax.experimental.pallas import tpu as pltpu
from jax.sharding import PartitionSpec as P

RING_Y = 4
WIDTHS = (128, 128, 128, 128)
ROWS_A = 160
LAG = 20
UNROLL = {128: 4, 256: 2, 384: 2}
SCHEDULE = (
    (0, "M", 0, 0), (0, "A", 2, 1), (0, "A", 1, 1), (0, "A", 3, 1), (0, "B", 0, 1), (0, "B", 2, 1), (0, "A", 0, 1),
    (0, "A", 4, 1), (0, "B", 1, 1), (2, "M", 0, 0), (2, "A", 2, 1), (2, "B", 0, 1), (2, "B", 2, 1), (2, "A", 3, 1),
    (2, "A", 0, 1), (0, "B", 0, 2), (0, "B", 1, 2), (2, "B", 1, 1), (0, "B", 2, 2), (0, "A", 1, 2), (1, "M", 0, 0),
    (1, "A", 1, 1), (1, "B", 2, 1), (1, "B", 1, 1), (1, "A", 0, 1), (2, "B", 0, 2), (0, "B", 0, 3), (2, "A", 2, 2),
    (2, "B", 2, 2), (0, "A", 0, 2), (1, "B", 0, 1), (3, "M", 0, 0), (3, "B", 1, 1), (3, "A", 0, 1), (3, "B", 2, 1),
    (3, "A", 1, 1), (3, "A", 4, 1), (3, "B", 0, 1), (2, "A", 4, 1), (1, "A", 4, 1), (1, "B", 1, 2), (2, "B", 0, 3),
    (1, "B", 2, 2), (1, "A", 2, 1), (0, "Z", 0, 1), (0, "B", 1, 3), (1, "A", 0, 2), (2, "A", 0, 2), (3, "B", 2, 2),
    (2, "A", 1, 1), (3, "B", 0, 2), (1, "A", 1, 2), (3, "B", 1, 2), (3, "A", 0, 2), (2, "B", 1, 2), (1, "B", 0, 2),
    (3, "B", 2, 3), (2, "B", 0, 4), (2, "A", 4, 2), (2, "A", 1, 2), (1, "B", 1, 3), (1, "Z", 0, 1), (3, "A", 2, 1),
    (2, "Z", 0, 1), (3, "B", 0, 3), (0, "A", 2, 2), (0, "Z", 0, 2), (3, "A", 1, 2), (1, "A", 3, 1), (3, "Z", 0, 1),
    (3, "A", 3, 1), (0, "B", 0, 4), (3, "B", 1, 3), (2, "Y", 0, 1), (2, "Z", 0, 2), (1, "Z", 0, 2), (1, "B", 0, 3),
    (1, "B", 1, 4), (2, "B", 2, 3), (0, "Y", 0, 1), (0, "B", 1, 4), (1, "A", 2, 2), (3, "Z", 0, 2), (3, "B", 0, 4),
    (1, "A", 3, 2), (2, "B", 1, 3), (1, "B", 0, 4), (0, "Z", 0, 3), (1, "B", 2, 3), (3, "A", 2, 2), (2, "A", 3, 2),
    (2, "Z", 0, 3), (3, "B", 1, 4), (3, "Y", 0, 1), (0, "A", 3, 2), (0, "B", 2, 3), (2, "B", 1, 4), (3, "Z", 0, 3),
    (1, "Z", 0, 3), (1, "Y", 0, 1), (3, "A", 3, 2), (2, "Z", 0, 4), (0, "Y", 0, 2), (0, "Z", 0, 4), (0, "B", 2, 4),
    (1, "A", 4, 2), (0, "A", 4, 2), (1, "Y", 0, 2), (2, "Y", 0, 2), (1, "B", 2, 4), (2, "B", 2, 4), (1, "Z", 0, 4),
    (3, "B", 2, 4), (3, "Y", 0, 2), (3, "Z", 0, 4), (3, "A", 4, 2), (0, "W", 0, 0), (0, "F", 0, 0), (1, "F", 0, 0),
    (2, "F", 0, 0), (3, "F", 0, 0),
)
F32 = jnp.float32
BF16 = jnp.bfloat16


class Ring:
    def __init__(self, n, peers, chunk, half, recv_half, recv_full, send_sem, recv_sem):
        self.n, self.last, self.peers, self.chunk, self.half = n, n // 2, peers, chunk, half
        self.recv_half, self.recv_full, self.send_sem, self.recv_sem = recv_half, recv_full, send_sem, recv_sem

    def offset(self, way, step):
        distance = self.last + 1 - step
        return distance if way == 0 else self.n - distance

    def slot(self, way, step):
        if step > 1:
            return self.recv_full(way, step - 2)
        return self.recv_half(way).at[pl.ds(0, self.source(way, 1).shape[0])]

    def source(self, way, step):
        source = self.chunk(self.offset(way, step))
        return self.half(source, way) if step == 1 else source

    def target(self, way, step):
        source = self.chunk(self.offset(way, step))
        return self.half(source, way) if step == 2 else source

    def copy(self, way, step):
        return pltpu.make_async_remote_copy(
            src_ref=self.source(way, step),
            dst_ref=self.slot(way, step),
            send_sem=self.send_sem.at[way, step - 1],
            recv_sem=self.recv_sem.at[way, step - 1],
            device_id={"rep": self.peers[way]},
            device_id_type=pl.DeviceIdType.MESH,
        )

    def send(self, way, step):
        self.copy(way, step).start()

    def arrived(self, way, step):
        self.copy(way, step).wait_recv()
        return self.slot(way, step)

    def drain(self, step):
        for way in (0, 1):
            self.copy(way, step).wait_send()


def halve(ref, which):
    size = ref.shape[0]
    first = size // 2 if size < 16 else (size // 16 + 1) // 2 * 16
    return ref.at[pl.ds(0, first)] if which == 0 else ref.at[pl.ds(first, size - first)]


def near_last(n):
    order = [n // 2]
    for distance in range(n // 2 - 1, 0, -1):
        order += [distance, n - distance]
    return order + [0]


def kernel(
    row_in, column_in, counts_in, features, tiles, degree_in, w_self, w_neigh, out,
    tiles_v, terms, partial, self_v, neigh_v, scale, acc, summed,
    ay_half, ay_full, az_half, az_full, bz_half, bz_full, by_half, by_full,
    ay_send, ay_recv, az_send, az_recv, bz_send, bz_recv, by_send, by_recv,
    halo_send, halo_recv, local_sem, found, links, row, column, counts, degree, mine, source,
):
    groups = len(WIDTHS)
    ring_z, ring_y, rows, _ = partial[0].shape
    slots, tile = tiles.shape[0], tiles.shape[1]
    steps = counts_in.shape[0]
    span = steps // 2
    capacity = slots // steps
    n_loop = lax.axis_size("loop")
    me_loop = lax.axis_index("loop")
    me = lax.axis_index("rep")
    y, z = lax.rem(me, ring_y), lax.div(me, ring_y)

    def at(zz, yy):
        return lax.rem(zz, ring_z) * ring_y + lax.rem(yy, ring_y)

    y_peers = (at(z, y + 1), at(z, y + ring_y - 1))
    z_peers = (at(z + 1, y), at(z + ring_z - 1, y))
    hops = [d * sign for d in range(1, span + 1) for sign in (1, -1)]
    turns = [span] + [span - d for d in hops]
    loop_peers = {d: lax.rem(me_loop + d + n_loop, n_loop) for d in hops}

    def place_of(h):
        return pl.ds(sum(WIDTHS[:h]), WIDTHS[h])

    def columns(h):
        return features.at[:, :, place_of(h)]

    own = [pltpu.make_async_copy(columns(h), mine[h], local_sem.at[h]) for h in range(groups)]
    moves = ((row_in, row), (degree_in, degree), (column_in, column), (counts_in, counts), (found, links), (tiles, tiles_v), (w_self, self_v), (w_neigh, neigh_v))
    row_copy, degree_copy, column_copy, counts_copy, link_copy, tile_copy, self_copy, neigh_copy = (
        pltpu.make_async_copy(src, dst, local_sem.at[groups + n]) for n, (src, dst) in enumerate(moves)
    )
    row_copy.start()
    own[0].start()

    barrier = pltpu.get_barrier_semaphore()
    for d in hops:
        pl.semaphore_signal(barrier, inc=1, device_id={"loop": loop_peers[d]}, device_id_type=pl.DeviceIdType.MESH)
    for peer in y_peers + z_peers:
        pl.semaphore_signal(barrier, inc=1, device_id={"rep": peer}, device_id_type=pl.DeviceIdType.MESH)
    for copy in (degree_copy, column_copy, counts_copy, tile_copy, *own[1:], self_copy, neigh_copy):
        copy.start()

    def link_slots():
        shape = (tile, tile)
        slot = lax.broadcasted_iota(jnp.int32, shape, 0)
        lane = lax.broadcasted_iota(jnp.int32, shape, 1)
        found[...] = jnp.full(found.shape, -1, jnp.int32)
        for place in range(steps):
            found[pl.ds(0, 1), pl.ds(place * capacity, capacity)] = row[:, pl.ds(turns[place] * capacity, capacity)]
        across = jnp.broadcast_to(found[pl.ds(0, 1), :], shape)
        down = across.astype(F32).T.astype(jnp.int32)
        before = jnp.where((down == across) & (slot < lane), slot + 1, 0)
        ending = jnp.where(down == lane, slot + 1, 0)
        found[pl.ds(0, 1), :] = jnp.max(before, axis=0, keepdims=True)
        found[pl.ds(1, 1), :] = jnp.max(ending, axis=0, keepdims=True)

    halo = [
        [
            pltpu.make_async_remote_copy(
                src_ref=mine[h],
                dst_ref=source[h][span - d],
                send_sem=halo_send.at[h, span - d],
                recv_sem=halo_recv.at[h, span - d],
                device_id={"loop": loop_peers[d]},
                device_id_type=pl.DeviceIdType.MESH,
            )
            for d in hops
        ]
        for h in range(groups)
    ]

    def start_halo(h):
        own[h].wait()
        for copy in halo[h]:
            copy.start()

    def multiply(h):
        width = WIDTHS[h]
        unroll = UNROLL[width]
        held = terms.at[:, :, pl.ds(0, width)]

        def some(turn, k, i, carry):
            block = mine[h] if turn == 0 else source[h][k]
            products = []
            for u in range(unroll):
                s = k * capacity + i * unroll + u
                products.append(jnp.dot(tiles_v[s], block[column[s]], preferred_element_type=F32))
            for u in range(unroll):
                c = i * unroll + u
                s = turn * capacity + c
                live = jnp.where(c < counts[k], 1.0, 0.0)
                held[s + 1] = products[u] * live + held[links[0, s]]
            return carry

        for turn, k in enumerate(turns):
            if turn > 0:
                halo[h][turn - 1].wait_recv()
            lax.fori_loop(0, capacity // unroll, functools.partial(some, turn, k), 0)

        def place(i, carry):
            zz, yy = lax.div(i, ring_y), lax.rem(i, ring_y)
            d = at(z + spot(zz, ring_z), y + spot(yy, ring_y))
            for t in range(rows // tile):
                term = held[links[1, d * (rows // tile) + t]]
                partial[h][zz, yy, pl.ds(t * tile, tile)] = term.astype(BF16)
            return carry

        lax.fori_loop(0, ring_z * ring_y, place, 0)

    def spot(i, n):
        distance = n // 2 - lax.div(i + 1, 2)
        return jnp.where(lax.rem(i, 2) == 1, distance, n - distance)

    order_z, order_y = near_last(ring_z), near_last(ring_y)
    sets_z = [(0, 1)] + [(2 * q - 1, 2) for q in range(1, ring_z // 2)] + [(ring_z - 1, 1)]
    sets_y = [(0, 1)] + [(2 * q - 1, 2) for q in range(1, ring_y // 2)] + [(ring_y - 1, 1)]
    rows_b = rows - ROWS_A
    in_a, in_b = pl.ds(0, ROWS_A), pl.ds(ROWS_A, rows_b)

    def rings(h):
        part = partial[h]

        def unit_a(q):
            first, count = sets_z[q]

            def chunk(o):
                yy = order_y.index(o)
                return part.at[pl.ds(first, 2), yy, in_a] if count == 2 else part.at[first, yy, in_a]

            def half(way):
                return ay_half[h].at[way, pl.ds(q, 1)] if count == 2 else ay_half[h].at[way, q]

            def full(way, step):
                return ay_full[h].at[way, pl.ds(first, 2)] if count == 2 else ay_full[h].at[way, first]

            return Ring(ring_y, y_peers, chunk, halve, half, full, ay_send.at[h, q], ay_recv.at[h, q])

        def unit_b(q):
            first, count = sets_y[q]

            def chunk(o):
                zz = order_z.index(o)
                return part.at[zz, pl.ds(first, 2), in_b] if count == 2 else part.at[zz, first, in_b]

            def half(way):
                return bz_half[h].at[way, pl.ds(q, 1)] if count == 2 else bz_half[h].at[way, q]

            def full(way, step):
                return bz_full[h].at[way, step, pl.ds(first, 2)] if count == 2 else bz_full[h].at[way, step, first]

            return Ring(ring_z, z_peers, chunk, halve, half, full, bz_send.at[h, q], bz_recv.at[h, q])

        az = Ring(
            ring_z, z_peers, lambda o: part.at[order_z.index(o), ring_y - 1, in_a], halve,
            lambda way: az_half[h].at[way], lambda way, step: az_full[h].at[way, step], az_send.at[h], az_recv.at[h],
        )
        by = Ring(
            ring_y, y_peers, lambda o: part.at[ring_z - 1, order_y.index(o), in_b], halve,
            lambda way: by_half[h].at[way], lambda way, step: by_full[h].at[way, step], by_send.at[h], by_recv.at[h],
        )
        return [unit_a(q) for q in range(len(sets_z))], [unit_b(q) for q in range(len(sets_y))], az, by

    made = [rings(h) for h in range(groups)]

    def forward(ring, step):
        for way in (0, 1):
            if step > 1:
                arrived = ring.arrived(way, step - 1)
                target = ring.target(way, step)
                target[...] = target[...] + arrived[...]
            ring.send(way, step)

    def second(ring, unit, step):
        sides = [unit.arrived(way, unit.last) for way in (0, 1)]
        for way in (0, 1):
            target = ring.chunk(ring.offset(way, step))
            if step == 1 and way == 1:
                ring.send(way, step)
                continue
            total = target[...].astype(F32)
            for side in sides:
                total += (side[way] if len(side.shape) == 3 else side[...]).astype(F32)
            if step > 1:
                arrived = ring.arrived(way, step - 1)
                if step == 2:
                    place = ring.target(way, 2)
                    target[...] = total.astype(BF16)
                    size = place.shape[0]
                    half = total[:size] if way == 0 else total[target.shape[0] - size :]
                    place[...] = (half + arrived[...].astype(F32)).astype(BF16)
                else:
                    target[...] = (total + arrived[...].astype(F32)).astype(BF16)
            else:
                target[...] = total.astype(BF16)
            ring.send(way, step)

    def last(ring, unit, rows_of, h):
        total = ring.chunk(0)[...].astype(F32)
        for way in (0, 1):
            total += unit.arrived(way, unit.last)[...].astype(F32)
        for way in (0, 1):
            total += ring.arrived(way, ring.last)[...].astype(F32)
        summed[rows_of, pl.ds(0, WIDTHS[h])] = total

    def run(h, name, q, step):
        units_a, units_b, az, by = made[h]
        if name == "A":
            forward(units_a[q], step)
        elif name == "B":
            forward(units_b[q], step)
        elif name == "Z":
            second(az, units_a[step - 1], step)
        elif name == "Y":
            second(by, units_b[step - 1], step)
        elif name == "M":
            multiply(h)
        elif name == "W":
            self_copy.wait()
            neigh_copy.wait()
            total = jnp.zeros(acc.shape, F32)
            for g in range(groups):
                total += jnp.dot(mine[g][...].reshape(rows, WIDTHS[g]), self_v[place_of(g)], preferred_element_type=F32)
            acc[...] = total
        elif name == "F":
            last(az, units_a[-1], in_a, h)
            last(by, units_b[-1], in_b, h)
            here = pl.ds(0, WIDTHS[h])
            mean = (summed[:, here] / scale[:, here]).astype(BF16)
            acc[...] += jnp.dot(mean, neigh_v[place_of(h)], preferred_element_type=F32)

    pl.semaphore_wait(barrier, len(hops) + 4)
    for h in range(groups):
        start_halo(h)
    row_copy.wait()
    link_slots()
    link_copy.start()
    terms[0] = jnp.zeros_like(terms[0])
    degree_copy.wait()
    for t in range(rows // tile):
        line = jnp.broadcast_to(degree[pl.ds(t, 1), :].astype(F32), (tile, tile))
        for c in range(max(WIDTHS) // tile):
            scale[pl.ds(t * tile, tile), pl.ds(c * tile, tile)] = line.T
    for copy in (link_copy, column_copy, counts_copy, tile_copy):
        copy.wait()
    flying = []
    for item in SCHEDULE:
        run(*item)
        h, name, q, step = item
        if name in "ABZY":
            units_a, units_b, az, by = made[h]
            flying.append(({"A": units_a, "B": units_b, "Z": [az], "Y": [by]}[name][q], step))
        if len(flying) > LAG:
            ring, sent = flying.pop(0)
            ring.drain(sent)
    out[...] = jnp.maximum(acc[...], 0.0).astype(out.dtype)

    for h in range(groups):
        for copy in halo[h]:
            copy.wait_send()
    for ring, sent in flying:
        ring.drain(sent)


def shards(features, tiles, slot_tile_row, slot_tile_column, counts, degree, w_self, w_neigh):
    rows, hidden = features.shape
    slots, tile = tiles.shape[0], tiles.shape[1]
    steps = counts.shape[0]
    ring_y = RING_Y
    ring_z = lax.axis_size("rep") // ring_y
    groups = len(WIDTHS)
    wide = max(WIDTHS)
    rows_b = rows - ROWS_A
    dma = pltpu.SemaphoreType.DMA

    def buffer(*shape):
        return [pltpu.VMEM((2, *shape, width), BF16) for width in WIDTHS]

    n_a, n_b = ring_z // 2 + 1, ring_y // 2 + 1
    last_y, last_z = ring_y // 2, ring_z // 2
    vmem = pl.BlockSpec(memory_space=pltpu.VMEM)
    anywhere = pl.BlockSpec(memory_space=pl.ANY)
    return pl.pallas_call(
        kernel,
        out_shape=jax.ShapeDtypeStruct((rows, hidden), BF16),
        in_specs=[anywhere] * 8,
        out_specs=vmem,
        scratch_shapes=[
            pltpu.VMEM((slots, tile, tile), BF16),
            pltpu.VMEM((slots + 1, tile, wide), F32),
            [pltpu.VMEM((ring_z, ring_y, rows, width), BF16) for width in WIDTHS],
            pltpu.VMEM(w_self.shape, BF16),
            pltpu.VMEM(w_neigh.shape, BF16),
            pltpu.VMEM((rows, wide), F32),
            pltpu.VMEM((rows, hidden), F32),
            pltpu.VMEM((rows, wide), F32),
            buffer(n_a, ROWS_A),
            buffer(ring_z, ROWS_A),
            buffer(ROWS_A),
            buffer(last_z - 1, ROWS_A),
            buffer(n_b, rows_b),
            buffer(last_z - 1, ring_y, rows_b),
            buffer(rows_b),
            buffer(last_y - 1, rows_b),
            *[dma((groups, n_a, 2, last_y))] * 2,
            *[dma((groups, 2, last_z))] * 2,
            *[dma((groups, n_b, 2, last_z))] * 2,
            *[dma((groups, 2, last_y))] * 2,
            dma((groups, steps)),
            dma((groups, steps)),
            dma((8 + groups,)),
            pltpu.VMEM((8, tile), jnp.int32),
            pltpu.SMEM((8, tile), jnp.int32),
            pltpu.VMEM((1, slots), jnp.int32),
            pltpu.SMEM((slots,), jnp.int32),
            pltpu.SMEM((steps,), jnp.int32),
            pltpu.VMEM((rows // tile, tile), jnp.int32),
            [pltpu.VMEM((rows // tile, tile, width), BF16) for width in WIDTHS],
            [[pltpu.VMEM((rows // tile, tile, width), BF16)] * steps for width in WIDTHS],
        ],
        compiler_params=pltpu.CompilerParams(
            collective_id=0, has_side_effects=True, vmem_limit_bytes=56 * 1024 * 1024
        ),
    )(
        slot_tile_row.reshape(1, slots),
        slot_tile_column,
        counts,
        features.reshape(rows // tile, tile, hidden),
        tiles,
        degree.reshape(rows // tile, tile),
        w_self,
        w_neigh,
    )


def solution(mesh):
    return jax.shard_map(
        shards,
        mesh=mesh,
        in_specs=(
            P(("loop", "rep"), None),
            P(("loop", "rep"), None, None),
            P(("loop", "rep")),
            P(("loop", "rep")),
            P(("loop", "rep")),
            P(("loop", "rep")),
            P(),
            P(),
        ),
        out_specs=P(("loop", "rep"), None),
        check_vma=False,
    )
```

```python
import functools

import jax
import jax.numpy as jnp
from jax import lax
from jax.experimental import pallas as pl
from jax.experimental.pallas import tpu as pltpu
from jax.sharding import PartitionSpec as P

RING_Y = 4
WIDTHS = (128, 128, 128, 128)
ROWS_A = 160
LAG = 20
UNROLL = {128: 4, 256: 2, 384: 2}
SCHEDULE = (
    (0, "M", 0, 0), (0, "B", 2, 1), (0, "A", 1, 1), (0, "B", 1, 1), (0, "A", 4, 1), (0, "A", 3, 1), (0, "A", 2, 1),
    (0, "A", 0, 1), (0, "B", 0, 1), (1, "M", 0, 0), (1, "A", 2, 1), (1, "A", 0, 1), (1, "B", 2, 1), (1, "B", 0, 1),
    (1, "A", 3, 1), (1, "A", 1, 1), (1, "B", 1, 1), (0, "B", 1, 2), (0, "B", 0, 2), (2, "M", 0, 0), (2, "A", 1, 1),
    (2, "A", 0, 1), (2, "B", 2, 1), (2, "A", 3, 1), (2, "B", 0, 1), (2, "B", 1, 1), (1, "B", 0, 2), (1, "B", 2, 2),
    (0, "A", 0, 2), (1, "B", 1, 2), (0, "B", 2, 2), (1, "A", 0, 2), (3, "M", 0, 0), (3, "B", 0, 1), (3, "A", 0, 1),
    (2, "A", 4, 1), (0, "B", 0, 3), (3, "B", 1, 1), (3, "B", 2, 1), (2, "A", 0, 2), (3, "A", 2, 1), (2, "A", 1, 2),
    (0, "A", 2, 2), (2, "B", 1, 2), (2, "B", 0, 2), (2, "B", 2, 2), (3, "A", 1, 1), (0, "B", 1, 3), (1, "A", 1, 2),
    (1, "B", 2, 3), (3, "B", 0, 2), (0, "B", 0, 4), (3, "A", 2, 2), (1, "Z", 0, 1), (3, "B", 2, 2), (3, "A", 0, 2),
    (2, "B", 0, 3), (2, "Z", 0, 1), (0, "A", 1, 2), (1, "A", 3, 2), (3, "B", 1, 2), (3, "B", 0, 3), (2, "B", 1, 3),
    (3, "B", 2, 3), (1, "B", 0, 3), (0, "Z", 0, 1), (2, "A", 2, 1), (3, "B", 1, 3), (3, "A", 4, 1), (3, "A", 1, 2),
    (1, "Z", 0, 2), (1, "B", 1, 3), (1, "A", 4, 1), (2, "Z", 0, 2), (3, "B", 0, 4), (1, "A", 2, 2), (3, "Z", 0, 1),
    (0, "Y", 0, 1), (2, "B", 0, 4), (0, "Z", 0, 2), (0, "B", 2, 3), (1, "B", 0, 4), (2, "A", 2, 2), (2, "B", 2, 3),
    (0, "B", 1, 4), (0, "A", 3, 2), (3, "Y", 0, 1), (3, "Z", 0, 2), (3, "B", 1, 4), (3, "A", 3, 1), (1, "B", 1, 4),
    (1, "Y", 0, 1), (2, "B", 1, 4), (0, "Y", 0, 2), (3, "B", 2, 4), (2, "Y", 0, 1), (2, "A", 3, 2), (0, "Z", 0, 3),
    (0, "A", 4, 2), (1, "Z", 0, 3), (3, "Z", 0, 3), (3, "A", 3, 2), (3, "A", 4, 2), (2, "Z", 0, 3), (1, "B", 2, 4),
    (0, "B", 2, 4), (1, "A", 4, 2), (1, "Y", 0, 2), (0, "Z", 0, 4), (2, "B", 2, 4), (2, "Y", 0, 2), (1, "Z", 0, 4),
    (2, "A", 4, 2), (2, "Z", 0, 4), (3, "Z", 0, 4), (3, "Y", 0, 2), (0, "W", 0, 0), (0, "F", 0, 0), (1, "F", 0, 0),
    (2, "F", 0, 0), (3, "F", 0, 0),
)
F32 = jnp.float32
BF16 = jnp.bfloat16


class Ring:
    def __init__(self, n, peers, chunk, half, recv_half, recv_full, send_sem, recv_sem):
        self.n, self.last, self.peers, self.chunk, self.half = n, n // 2, peers, chunk, half
        self.recv_half, self.recv_full, self.send_sem, self.recv_sem = recv_half, recv_full, send_sem, recv_sem

    def offset(self, way, step):
        distance = self.last + 1 - step
        return distance if way == 0 else self.n - distance

    def slot(self, way, step):
        if step > 1:
            return self.recv_full(way, step - 2)
        return self.recv_half(way).at[pl.ds(0, self.source(way, 1).shape[0])]

    def source(self, way, step):
        source = self.chunk(self.offset(way, step))
        return self.half(source, way) if step == 1 else source

    def target(self, way, step):
        source = self.chunk(self.offset(way, step))
        return self.half(source, way) if step == 2 else source

    def copy(self, way, step):
        return pltpu.make_async_remote_copy(
            src_ref=self.source(way, step),
            dst_ref=self.slot(way, step),
            send_sem=self.send_sem.at[way, step - 1],
            recv_sem=self.recv_sem.at[way, step - 1],
            device_id={"rep": self.peers[way]},
            device_id_type=pl.DeviceIdType.MESH,
        )

    def send(self, way, step):
        self.copy(way, step).start()

    def arrived(self, way, step):
        self.copy(way, step).wait_recv()
        return self.slot(way, step)

    def drain(self, step):
        for way in (0, 1):
            self.copy(way, step).wait_send()


def halve(ref, which):
    size = ref.shape[0]
    first = size // 2 if size < 16 else (size // 16 + 1) // 2 * 16
    return ref.at[pl.ds(0, first)] if which == 0 else ref.at[pl.ds(first, size - first)]


def near_last(n):
    order = [n // 2]
    for distance in range(n // 2 - 1, 0, -1):
        order += [distance, n - distance]
    return order + [0]


def kernel(
    row_in, column_in, counts_in, features, tiles, degree_in, w_self, w_neigh, out,
    tiles_v, terms, partial, self_v, neigh_v, scale, acc, summed,
    ay_half, ay_full, az_half, az_full, bz_half, bz_full, by_half, by_full,
    ay_send, ay_recv, az_send, az_recv, bz_send, bz_recv, by_send, by_recv,
    halo_send, halo_recv, local_sem, found, links, row, column, counts, degree, mine, source,
):
    groups = len(WIDTHS)
    ring_z, ring_y, rows, _ = partial[0].shape
    slots, tile = tiles.shape[0], tiles.shape[1]
    steps = counts_in.shape[0]
    span = steps // 2
    capacity = slots // steps
    n_loop = lax.axis_size("loop")
    me_loop = lax.axis_index("loop")
    me = lax.axis_index("rep")
    y, z = lax.rem(me, ring_y), lax.div(me, ring_y)

    def at(zz, yy):
        return lax.rem(zz, ring_z) * ring_y + lax.rem(yy, ring_y)

    y_peers = (at(z, y + 1), at(z, y + ring_y - 1))
    z_peers = (at(z + 1, y), at(z + ring_z - 1, y))
    hops = [d * sign for d in range(1, span + 1) for sign in (1, -1)]
    turns = [span] + [span - d for d in hops]
    loop_peers = {d: lax.rem(me_loop + d + n_loop, n_loop) for d in hops}

    def place_of(h):
        return pl.ds(sum(WIDTHS[:h]), WIDTHS[h])

    def columns(h):
        return features.at[:, :, place_of(h)]

    own = [pltpu.make_async_copy(columns(h), mine[h], local_sem.at[h]) for h in range(groups)]
    moves = ((row_in, row), (degree_in, degree), (column_in, column), (counts_in, counts), (found, links), (tiles, tiles_v), (w_self, self_v), (w_neigh, neigh_v))
    row_copy, degree_copy, column_copy, counts_copy, link_copy, tile_copy, self_copy, neigh_copy = (
        pltpu.make_async_copy(src, dst, local_sem.at[groups + n]) for n, (src, dst) in enumerate(moves)
    )
    row_copy.start()
    own[0].start()

    barrier = pltpu.get_barrier_semaphore()
    for d in hops:
        pl.semaphore_signal(barrier, inc=1, device_id={"loop": loop_peers[d]}, device_id_type=pl.DeviceIdType.MESH)
    for peer in y_peers + z_peers:
        pl.semaphore_signal(barrier, inc=1, device_id={"rep": peer}, device_id_type=pl.DeviceIdType.MESH)
    for copy in (degree_copy, column_copy, counts_copy, tile_copy, *own[1:], self_copy, neigh_copy):
        copy.start()

    def link_slots():
        shape = (tile, tile)
        slot = lax.broadcasted_iota(jnp.int32, shape, 0)
        lane = lax.broadcasted_iota(jnp.int32, shape, 1)
        found[...] = jnp.full(found.shape, -1, jnp.int32)
        for place in range(steps):
            found[pl.ds(0, 1), pl.ds(place * capacity, capacity)] = row[:, pl.ds(turns[place] * capacity, capacity)]
        across = jnp.broadcast_to(found[pl.ds(0, 1), :], shape)
        down = across.astype(F32).T.astype(jnp.int32)
        before = jnp.where((down == across) & (slot < lane), slot + 1, 0)
        ending = jnp.where(down == lane, slot + 1, 0)
        found[pl.ds(0, 1), :] = jnp.max(before, axis=0, keepdims=True)
        found[pl.ds(1, 1), :] = jnp.max(ending, axis=0, keepdims=True)

    halo = [
        [
            pltpu.make_async_remote_copy(
                src_ref=mine[h],
                dst_ref=source[h][span - d],
                send_sem=halo_send.at[h, span - d],
                recv_sem=halo_recv.at[h, span - d],
                device_id={"loop": loop_peers[d]},
                device_id_type=pl.DeviceIdType.MESH,
            )
            for d in hops
        ]
        for h in range(groups)
    ]

    def start_halo(h):
        own[h].wait()
        for copy in halo[h]:
            copy.start()

    def multiply(h):
        width = WIDTHS[h]
        unroll = UNROLL[width]
        held = terms.at[:, :, pl.ds(0, width)]

        def some(turn, k, i, carry):
            block = mine[h] if turn == 0 else source[h][k]
            products = []
            for u in range(unroll):
                s = k * capacity + i * unroll + u
                products.append(jnp.dot(tiles_v[s], block[column[s]], preferred_element_type=F32))
            for u in range(unroll):
                c = i * unroll + u
                s = turn * capacity + c
                live = jnp.where(c < counts[k], 1.0, 0.0)
                held[s + 1] = products[u] * live + held[links[0, s]]
            return carry

        for turn, k in enumerate(turns):
            if turn > 0:
                halo[h][turn - 1].wait_recv()
            if turn == 3 and h == 0:
                start_halo(1)
            lax.fori_loop(0, capacity // unroll, functools.partial(some, turn, k), 0)

        if h + 2 < groups:
            start_halo(h + 2)

        def place(i, carry):
            zz, yy = lax.div(i, ring_y), lax.rem(i, ring_y)
            d = at(z + spot(zz, ring_z), y + spot(yy, ring_y))
            for t in range(rows // tile):
                term = held[links[1, d * (rows // tile) + t]]
                partial[h][zz, yy, pl.ds(t * tile, tile)] = term.astype(BF16)
            return carry

        if h > 0:
            lax.fori_loop(0, ring_z * ring_y, place, 0)
        else:
            for unit, (first, count) in zip(made[h][0], sets_z):
                lax.fori_loop(first * ring_y, (first + count) * ring_y, place, 0)
                forward(unit, 1)

    def spot(i, n):
        distance = n // 2 - lax.div(i + 1, 2)
        return jnp.where(lax.rem(i, 2) == 1, distance, n - distance)

    order_z, order_y = near_last(ring_z), near_last(ring_y)
    sets_z = [(0, 1)] + [(2 * q - 1, 2) for q in range(1, ring_z // 2)] + [(ring_z - 1, 1)]
    sets_y = [(0, 1)] + [(2 * q - 1, 2) for q in range(1, ring_y // 2)] + [(ring_y - 1, 1)]
    rows_b = rows - ROWS_A
    in_a, in_b = pl.ds(0, ROWS_A), pl.ds(ROWS_A, rows_b)

    def rings(h):
        part = partial[h]

        def unit_a(q):
            first, count = sets_z[q]

            def chunk(o):
                yy = order_y.index(o)
                return part.at[pl.ds(first, 2), yy, in_a] if count == 2 else part.at[first, yy, in_a]

            def half(way):
                return ay_half[h].at[way, pl.ds(q, 1)] if count == 2 else ay_half[h].at[way, q]

            def full(way, step):
                return ay_full[h].at[way, pl.ds(first, 2)] if count == 2 else ay_full[h].at[way, first]

            return Ring(ring_y, y_peers, chunk, halve, half, full, ay_send.at[h, q], ay_recv.at[h, q])

        def unit_b(q):
            first, count = sets_y[q]

            def chunk(o):
                zz = order_z.index(o)
                return part.at[zz, pl.ds(first, 2), in_b] if count == 2 else part.at[zz, first, in_b]

            def half(way):
                return bz_half[h].at[way, pl.ds(q, 1)] if count == 2 else bz_half[h].at[way, q]

            def full(way, step):
                return bz_full[h].at[way, step, pl.ds(first, 2)] if count == 2 else bz_full[h].at[way, step, first]

            return Ring(ring_z, z_peers, chunk, halve, half, full, bz_send.at[h, q], bz_recv.at[h, q])

        az = Ring(
            ring_z, z_peers, lambda o: part.at[order_z.index(o), ring_y - 1, in_a], halve,
            lambda way: az_half[h].at[way], lambda way, step: az_full[h].at[way, step], az_send.at[h], az_recv.at[h],
        )
        by = Ring(
            ring_y, y_peers, lambda o: part.at[ring_z - 1, order_y.index(o), in_b], halve,
            lambda way: by_half[h].at[way], lambda way, step: by_full[h].at[way, step], by_send.at[h], by_recv.at[h],
        )
        return [unit_a(q) for q in range(len(sets_z))], [unit_b(q) for q in range(len(sets_y))], az, by

    made = [rings(h) for h in range(groups)]

    def forward(ring, step):
        for way in (0, 1):
            if step > 1:
                arrived = ring.arrived(way, step - 1)
                target = ring.target(way, step)
                target[...] = target[...] + arrived[...]
            ring.send(way, step)

    def second(ring, unit, step):
        sides = [unit.arrived(way, unit.last) for way in (0, 1)]
        for way in (0, 1):
            target = ring.chunk(ring.offset(way, step))
            if step == 1 and way == 1:
                ring.send(way, step)
                continue
            total = target[...].astype(F32)
            for side in sides:
                total += (side[way] if len(side.shape) == 3 else side[...]).astype(F32)
            if step > 1:
                arrived = ring.arrived(way, step - 1)
                if step == 2:
                    place = ring.target(way, 2)
                    target[...] = total.astype(BF16)
                    size = place.shape[0]
                    half = total[:size] if way == 0 else total[target.shape[0] - size :]
                    place[...] = (half + arrived[...].astype(F32)).astype(BF16)
                else:
                    target[...] = (total + arrived[...].astype(F32)).astype(BF16)
            else:
                target[...] = total.astype(BF16)
            ring.send(way, step)

    def last(ring, unit, rows_of, h):
        total = ring.chunk(0)[...].astype(F32)
        for way in (0, 1):
            total += unit.arrived(way, unit.last)[...].astype(F32)
        for way in (0, 1):
            total += ring.arrived(way, ring.last)[...].astype(F32)
        summed[rows_of, pl.ds(0, WIDTHS[h])] = total

    def run(h, name, q, step):
        units_a, units_b, az, by = made[h]
        if name == "A" and (h, step) == (0, 1):
            pass
        elif name == "A":
            forward(units_a[q], step)
        elif name == "B":
            forward(units_b[q], step)
        elif name == "Z":
            second(az, units_a[step - 1], step)
        elif name == "Y":
            second(by, units_b[step - 1], step)
        elif name == "M":
            multiply(h)
        elif name == "W":
            self_copy.wait()
            neigh_copy.wait()
            total = jnp.zeros(acc.shape, F32)
            for g in range(groups):
                total += jnp.dot(mine[g][...].reshape(rows, WIDTHS[g]), self_v[place_of(g)], preferred_element_type=F32)
            acc[...] = total
        elif name == "F":
            last(az, units_a[-1], in_a, h)
            last(by, units_b[-1], in_b, h)
            here = pl.ds(0, WIDTHS[h])
            mean = (summed[:, here] / scale[:, here]).astype(BF16)
            acc[...] += jnp.dot(mean, neigh_v[place_of(h)], preferred_element_type=F32)

    pl.semaphore_wait(barrier, len(hops) + 4)
    start_halo(0)
    row_copy.wait()
    link_slots()
    link_copy.start()
    terms[0] = jnp.zeros_like(terms[0])
    degree_copy.wait()
    for t in range(rows // tile):
        line = jnp.broadcast_to(degree[pl.ds(t, 1), :].astype(F32), (tile, tile))
        for c in range(max(WIDTHS) // tile):
            scale[pl.ds(t * tile, tile), pl.ds(c * tile, tile)] = line.T
    for copy in (link_copy, column_copy, counts_copy, tile_copy):
        copy.wait()
    flying = []
    for item in SCHEDULE:
        run(*item)
        h, name, q, step = item
        if name in "ABZY":
            units_a, units_b, az, by = made[h]
            flying.append(({"A": units_a, "B": units_b, "Z": [az], "Y": [by]}[name][q], step))
        if len(flying) > LAG:
            ring, sent = flying.pop(0)
            ring.drain(sent)
    out[...] = jnp.maximum(acc[...], 0.0).astype(out.dtype)

    for h in range(groups):
        for copy in halo[h]:
            copy.wait_send()
    for ring, sent in flying:
        ring.drain(sent)


def shards(features, tiles, slot_tile_row, slot_tile_column, counts, degree, w_self, w_neigh):
    rows, hidden = features.shape
    slots, tile = tiles.shape[0], tiles.shape[1]
    steps = counts.shape[0]
    ring_y = RING_Y
    ring_z = lax.axis_size("rep") // ring_y
    groups = len(WIDTHS)
    wide = max(WIDTHS)
    rows_b = rows - ROWS_A
    dma = pltpu.SemaphoreType.DMA

    def buffer(*shape):
        return [pltpu.VMEM((2, *shape, width), BF16) for width in WIDTHS]

    n_a, n_b = ring_z // 2 + 1, ring_y // 2 + 1
    last_y, last_z = ring_y // 2, ring_z // 2
    vmem = pl.BlockSpec(memory_space=pltpu.VMEM)
    anywhere = pl.BlockSpec(memory_space=pl.ANY)
    return pl.pallas_call(
        kernel,
        out_shape=jax.ShapeDtypeStruct((rows, hidden), BF16),
        in_specs=[anywhere] * 8,
        out_specs=vmem,
        scratch_shapes=[
            pltpu.VMEM((slots, tile, tile), BF16),
            pltpu.VMEM((slots + 1, tile, wide), F32),
            [pltpu.VMEM((ring_z, ring_y, rows, width), BF16) for width in WIDTHS],
            pltpu.VMEM(w_self.shape, BF16),
            pltpu.VMEM(w_neigh.shape, BF16),
            pltpu.VMEM((rows, wide), F32),
            pltpu.VMEM((rows, hidden), F32),
            pltpu.VMEM((rows, wide), F32),
            buffer(n_a, ROWS_A),
            buffer(ring_z, ROWS_A),
            buffer(ROWS_A),
            buffer(last_z - 1, ROWS_A),
            buffer(n_b, rows_b),
            buffer(last_z - 1, ring_y, rows_b),
            buffer(rows_b),
            buffer(last_y - 1, rows_b),
            *[dma((groups, n_a, 2, last_y))] * 2,
            *[dma((groups, 2, last_z))] * 2,
            *[dma((groups, n_b, 2, last_z))] * 2,
            *[dma((groups, 2, last_y))] * 2,
            dma((groups, steps)),
            dma((groups, steps)),
            dma((8 + groups,)),
            pltpu.VMEM((8, tile), jnp.int32),
            pltpu.SMEM((8, tile), jnp.int32),
            pltpu.VMEM((1, slots), jnp.int32),
            pltpu.SMEM((slots,), jnp.int32),
            pltpu.SMEM((steps,), jnp.int32),
            pltpu.VMEM((rows // tile, tile), jnp.int32),
            [pltpu.VMEM((rows // tile, tile, width), BF16) for width in WIDTHS],
            [[pltpu.VMEM((rows // tile, tile, width), BF16)] * steps for width in WIDTHS],
        ],
        compiler_params=pltpu.CompilerParams(
            collective_id=0, has_side_effects=True, vmem_limit_bytes=56 * 1024 * 1024
        ),
    )(
        slot_tile_row.reshape(1, slots),
        slot_tile_column,
        counts,
        features.reshape(rows // tile, tile, hidden),
        tiles,
        degree.reshape(rows // tile, tile),
        w_self,
        w_neigh,
    )


def solution(mesh):
    return jax.shard_map(
        shards,
        mesh=mesh,
        in_specs=(
            P(("loop", "rep"), None),
            P(("loop", "rep"), None, None),
            P(("loop", "rep")),
            P(("loop", "rep")),
            P(("loop", "rep")),
            P(("loop", "rep")),
            P(),
            P(),
        ),
        out_specs=P(("loop", "rep"), None),
        check_vma=False,
    )
```

```python
import functools

import jax
import jax.numpy as jnp
from jax import lax
from jax.experimental import pallas as pl
from jax.experimental.pallas import tpu as pltpu
from jax.sharding import PartitionSpec as P

RING_Y = 4
WIDTHS = (128, 128, 128, 128)
ROWS_A = 160
LAG = 20
UNROLL = {128: 4, 256: 2, 384: 2}
SCHEDULE = (
    (0, "M", 0, 0), (0, "A", 1, 1), (0, "B", 2, 1), (0, "A", 3, 1), (0, "A", 0, 1), (0, "B", 0, 1), (0, "B", 1, 1),
    (0, "A", 4, 1), (1, "M", 0, 0), (1, "A", 0, 1), (1, "A", 1, 1), (1, "B", 1, 1), (1, "B", 2, 1), (1, "B", 0, 1),
    (1, "A", 3, 1), (0, "B", 2, 2), (0, "A", 1, 2), (0, "B", 0, 2), (0, "B", 1, 2), (2, "M", 0, 0), (2, "A", 0, 1),
    (2, "B", 1, 1), (1, "A", 1, 2), (2, "B", 2, 1), (2, "B", 0, 1), (1, "A", 0, 2), (0, "B", 2, 3), (1, "B", 2, 2),
    (1, "B", 0, 2), (1, "B", 1, 2), (2, "A", 1, 1), (3, "M", 0, 0), (3, "A", 3, 1), (3, "B", 0, 1), (3, "A", 2, 1),
    (3, "A", 0, 1), (3, "B", 2, 1), (3, "B", 1, 1), (2, "B", 0, 2), (3, "A", 1, 1), (0, "A", 0, 2), (1, "B", 0, 3),
    (2, "B", 1, 2), (1, "B", 1, 3), (2, "B", 2, 2), (3, "B", 2, 2), (2, "A", 0, 2), (0, "B", 0, 3), (3, "B", 1, 2),
    (0, "A", 2, 1), (2, "B", 0, 3), (2, "A", 1, 2), (3, "A", 0, 2), (2, "A", 2, 1), (3, "A", 1, 2), (1, "Z", 0, 1),
    (2, "A", 4, 1), (1, "A", 4, 1), (3, "B", 0, 2), (2, "A", 3, 1), (0, "B", 1, 3), (0, "Z", 0, 1), (1, "A", 2, 1),
    (2, "B", 1, 3), (2, "B", 0, 4), (3, "B", 2, 3), (0, "A", 2, 2), (3, "A", 2, 2), (1, "A", 3, 2), (3, "B", 0, 3),
    (1, "B", 0, 4), (3, "Z", 0, 1), (0, "B", 0, 4), (1, "B", 2, 3), (0, "Z", 0, 2), (0, "B", 1, 4), (2, "Z", 0, 1),
    (3, "Z", 0, 2), (1, "Y", 0, 1), (2, "B", 2, 3), (2, "B", 1, 4), (3, "A", 3, 2), (1, "A", 2, 2), (1, "Z", 0, 2),
    (2, "A", 2, 2), (1, "B", 1, 4), (0, "Z", 0, 3), (3, "Z", 0, 3), (3, "A", 4, 1), (2, "Z", 0, 2), (0, "A", 3, 2),
    (0, "Y", 0, 1), (3, "B", 1, 3), (2, "A", 3, 2), (3, "B", 0, 4), (2, "B", 2, 4), (1, "Z", 0, 3), (2, "Y", 0, 1),
    (1, "A", 4, 2), (0, "B", 2, 4), (2, "Z", 0, 3), (3, "B", 1, 4), (3, "Y", 0, 1), (0, "Z", 0, 4), (3, "B", 2, 4),
    (0, "A", 4, 2), (1, "Y", 0, 2), (1, "Z", 0, 4), (0, "Y", 0, 2), (2, "A", 4, 2), (2, "Y", 0, 2), (3, "A", 4, 2),
    (1, "B", 2, 4), (2, "Z", 0, 4), (3, "Y", 0, 2), (3, "Z", 0, 4), (0, "W", 0, 0), (0, "F", 0, 0), (1, "F", 0, 0),
    (2, "F", 0, 0), (3, "F", 0, 0),
)
F32 = jnp.float32
BF16 = jnp.bfloat16


class Ring:
    def __init__(self, n, peers, chunk, half, recv_half, recv_full, send_sem, recv_sem):
        self.n, self.last, self.peers, self.chunk, self.half = n, n // 2, peers, chunk, half
        self.recv_half, self.recv_full, self.send_sem, self.recv_sem = recv_half, recv_full, send_sem, recv_sem

    def offset(self, way, step):
        distance = self.last + 1 - step
        return distance if way == 0 else self.n - distance

    def slot(self, way, step):
        if step > 1:
            return self.recv_full(way, step - 2)
        return self.recv_half(way).at[pl.ds(0, self.source(way, 1).shape[0])]

    def source(self, way, step):
        source = self.chunk(self.offset(way, step))
        return self.half(source, way) if step == 1 else source

    def target(self, way, step):
        source = self.chunk(self.offset(way, step))
        return self.half(source, way) if step == 2 else source

    def copy(self, way, step):
        return pltpu.make_async_remote_copy(
            src_ref=self.source(way, step),
            dst_ref=self.slot(way, step),
            send_sem=self.send_sem.at[way, step - 1],
            recv_sem=self.recv_sem.at[way, step - 1],
            device_id={"rep": self.peers[way]},
            device_id_type=pl.DeviceIdType.MESH,
        )

    def send(self, way, step):
        self.copy(way, step).start()

    def arrived(self, way, step):
        self.copy(way, step).wait_recv()
        return self.slot(way, step)

    def drain(self, step):
        for way in (0, 1):
            self.copy(way, step).wait_send()


def halve(ref, which):
    size = ref.shape[0]
    first = size // 2 if size < 16 else (size // 16 + 1) // 2 * 16
    return ref.at[pl.ds(0, first)] if which == 0 else ref.at[pl.ds(first, size - first)]


def near_last(n):
    order = [n // 2]
    for distance in range(n // 2 - 1, 0, -1):
        order += [distance, n - distance]
    return order + [0]


def kernel(
    row_in, column_in, counts_in, features, tiles, degree_in, w_self, w_neigh, out,
    tiles_v, terms, partial, self_v, neigh_v, scale, acc, summed,
    ay_half, ay_full, az_half, az_full, bz_half, bz_full, by_half, by_full,
    ay_send, ay_recv, az_send, az_recv, bz_send, bz_recv, by_send, by_recv,
    halo_send, halo_recv, local_sem, found, links, row, column, counts, degree, mine, source,
):
    groups = len(WIDTHS)
    ring_z, ring_y, rows, _ = partial[0].shape
    slots, tile = tiles.shape[0], tiles.shape[1]
    steps = counts_in.shape[0]
    span = steps // 2
    capacity = slots // steps
    n_loop = lax.axis_size("loop")
    me_loop = lax.axis_index("loop")
    me = lax.axis_index("rep")
    y, z = lax.rem(me, ring_y), lax.div(me, ring_y)

    def at(zz, yy):
        return lax.rem(zz, ring_z) * ring_y + lax.rem(yy, ring_y)

    y_peers = (at(z, y + 1), at(z, y + ring_y - 1))
    z_peers = (at(z + 1, y), at(z + ring_z - 1, y))
    hops = [d * sign for d in range(1, span + 1) for sign in (1, -1)]
    turns = [span] + [span - d for d in hops]
    loop_peers = {d: lax.rem(me_loop + d + n_loop, n_loop) for d in hops}

    def place_of(h):
        return pl.ds(sum(WIDTHS[:h]), WIDTHS[h])

    def columns(h):
        return features.at[:, :, place_of(h)]

    own = [pltpu.make_async_copy(columns(h), mine[h], local_sem.at[h]) for h in range(groups)]
    moves = ((row_in, row), (degree_in, degree), (column_in, column), (counts_in, counts), (found, links), (tiles, tiles_v), (w_self, self_v), (w_neigh, neigh_v))
    row_copy, degree_copy, column_copy, counts_copy, link_copy, tile_copy, self_copy, neigh_copy = (
        pltpu.make_async_copy(src, dst, local_sem.at[groups + n]) for n, (src, dst) in enumerate(moves)
    )
    row_copy.start()
    own[0].start()

    barrier = pltpu.get_barrier_semaphore()
    for d in hops:
        pl.semaphore_signal(barrier, inc=1, device_id={"loop": loop_peers[d]}, device_id_type=pl.DeviceIdType.MESH)
    for peer in y_peers + z_peers:
        pl.semaphore_signal(barrier, inc=1, device_id={"rep": peer}, device_id_type=pl.DeviceIdType.MESH)
    for copy in (degree_copy, column_copy, counts_copy, tile_copy, *own[1:], self_copy, neigh_copy):
        copy.start()

    def link_slots():
        shape = (tile, tile)
        slot = lax.broadcasted_iota(jnp.int32, shape, 0)
        lane = lax.broadcasted_iota(jnp.int32, shape, 1)
        found[...] = jnp.full(found.shape, -1, jnp.int32)
        for place in range(steps):
            found[pl.ds(0, 1), pl.ds(place * capacity, capacity)] = row[:, pl.ds(turns[place] * capacity, capacity)]
        across = jnp.broadcast_to(found[pl.ds(0, 1), :], shape)
        down = across.astype(F32).T.astype(jnp.int32)
        before = jnp.where((down == across) & (slot < lane), slot + 1, 0)
        ending = jnp.where(down == lane, slot + 1, 0)
        found[pl.ds(0, 1), :] = jnp.max(before, axis=0, keepdims=True)
        found[pl.ds(1, 1), :] = jnp.max(ending, axis=0, keepdims=True)

    halo = [
        [
            pltpu.make_async_remote_copy(
                src_ref=mine[h],
                dst_ref=source[h][span - d],
                send_sem=halo_send.at[h, span - d],
                recv_sem=halo_recv.at[h, span - d],
                device_id={"loop": loop_peers[d]},
                device_id_type=pl.DeviceIdType.MESH,
            )
            for d in hops
        ]
        for h in range(groups)
    ]

    def start_halo(h):
        own[h].wait()
        for copy in halo[h]:
            copy.start()

    def multiply(h):
        width = WIDTHS[h]
        unroll = UNROLL[width]
        held = terms.at[:, :, pl.ds(0, width)]

        def some(turn, k, i, carry):
            block = mine[h] if turn == 0 else source[h][k]
            products = []
            for u in range(unroll):
                s = k * capacity + i * unroll + u
                products.append(jnp.dot(tiles_v[s], block[column[s]], preferred_element_type=F32))
            for u in range(unroll):
                c = i * unroll + u
                s = turn * capacity + c
                live = jnp.where(c < counts[k], 1.0, 0.0)
                held[s + 1] = products[u] * live + held[links[0, s]]
            return carry

        for turn, k in enumerate(turns):
            if turn > 0:
                halo[h][turn - 1].wait_recv()
            if turn == 3 and h == 0:
                start_halo(1)
            lax.fori_loop(0, capacity // unroll, functools.partial(some, turn, k), 0)

        if h + 2 < groups:
            start_halo(h + 2)

        def place(i, carry):
            zz, yy = lax.div(i, ring_y), lax.rem(i, ring_y)
            d = at(z + spot(zz, ring_z), y + spot(yy, ring_y))
            for t in range(rows // tile):
                term = held[links[1, d * (rows // tile) + t]]
                partial[h][zz, yy, pl.ds(t * tile, tile)] = term.astype(BF16)
            return carry

        if h > 0:
            lax.fori_loop(0, ring_z * ring_y, place, 0)
        else:
            for unit, (first, count) in zip(made[h][0], sets_z):
                lax.fori_loop(first * ring_y, (first + count) * ring_y, place, 0)
                forward(unit, 1)

    def spot(i, n):
        distance = n // 2 - lax.div(i + 1, 2)
        return jnp.where(lax.rem(i, 2) == 1, distance, n - distance)

    order_z, order_y = near_last(ring_z), near_last(ring_y)
    sets_z = [(0, 1)] + [(2 * q - 1, 2) for q in range(1, ring_z // 2)] + [(ring_z - 1, 1)]
    sets_y = [(0, 1)] + [(2 * q - 1, 2) for q in range(1, ring_y // 2)] + [(ring_y - 1, 1)]
    rows_b = rows - ROWS_A
    in_a, in_b = pl.ds(0, ROWS_A), pl.ds(ROWS_A, rows_b)

    def rings(h):
        part = partial[h]

        def unit_a(q):
            first, count = sets_z[q]

            def chunk(o):
                yy = order_y.index(o)
                return part.at[pl.ds(first, 2), yy, in_a] if count == 2 else part.at[first, yy, in_a]

            def half(way):
                return ay_half[h].at[way, pl.ds(q, 1)] if count == 2 else ay_half[h].at[way, q]

            def full(way, step):
                return ay_full[h].at[way, pl.ds(first, 2)] if count == 2 else ay_full[h].at[way, first]

            return Ring(ring_y, y_peers, chunk, halve, half, full, ay_send.at[h, q], ay_recv.at[h, q])

        def unit_b(q):
            first, count = sets_y[q]

            def chunk(o):
                zz = order_z.index(o)
                return part.at[zz, pl.ds(first, 2), in_b] if count == 2 else part.at[zz, first, in_b]

            def half(way):
                return bz_half[h].at[way, pl.ds(q, 1)] if count == 2 else bz_half[h].at[way, q]

            def full(way, step):
                return bz_full[h].at[way, step, pl.ds(first, 2)] if count == 2 else bz_full[h].at[way, step, first]

            return Ring(ring_z, z_peers, chunk, halve, half, full, bz_send.at[h, q], bz_recv.at[h, q])

        az = Ring(
            ring_z, z_peers, lambda o: part.at[order_z.index(o), ring_y - 1, in_a], halve,
            lambda way: az_half[h].at[way], lambda way, step: az_full[h].at[way, step], az_send.at[h], az_recv.at[h],
        )
        by = Ring(
            ring_y, y_peers, lambda o: part.at[ring_z - 1, order_y.index(o), in_b], halve,
            lambda way: by_half[h].at[way], lambda way, step: by_full[h].at[way, step], by_send.at[h], by_recv.at[h],
        )
        return [unit_a(q) for q in range(len(sets_z))], [unit_b(q) for q in range(len(sets_y))], az, by

    made = [rings(h) for h in range(groups)]

    def forward(ring, step):
        for way in (0, 1):
            if step > 1:
                arrived = ring.arrived(way, step - 1)
                target = ring.target(way, step)
                target[...] = target[...] + arrived[...]
            ring.send(way, step)

    def second(ring, unit, step):
        sides = [unit.arrived(way, unit.last) for way in (0, 1)]
        for way in (0, 1):
            target = ring.chunk(ring.offset(way, step))
            if step == 1 and way == 1:
                ring.send(way, step)
                continue
            total = target[...].astype(F32)
            for side in sides:
                total += (side[way] if len(side.shape) == 3 else side[...]).astype(F32)
            if step > 1:
                arrived = ring.arrived(way, step - 1)
                if step == 2:
                    place = ring.target(way, 2)
                    target[...] = total.astype(BF16)
                    size = place.shape[0]
                    half = total[:size] if way == 0 else total[target.shape[0] - size :]
                    place[...] = (half + arrived[...].astype(F32)).astype(BF16)
                else:
                    target[...] = (total + arrived[...].astype(F32)).astype(BF16)
            else:
                target[...] = total.astype(BF16)
            ring.send(way, step)

    def last(ring, unit, rows_of, h):
        total = ring.chunk(0)[...].astype(F32)
        for way in (0, 1):
            total += unit.arrived(way, unit.last)[...].astype(F32)
        for way in (0, 1):
            total += ring.arrived(way, ring.last)[...].astype(F32)
        summed[rows_of, pl.ds(0, WIDTHS[h])] = total

    def run(h, name, q, step):
        units_a, units_b, az, by = made[h]
        if name == "A" and (h, step) == (0, 1):
            pass
        elif name == "A":
            forward(units_a[q], step)
        elif name == "B":
            forward(units_b[q], step)
        elif name == "Z":
            second(az, units_a[step - 1], step)
        elif name == "Y":
            second(by, units_b[step - 1], step)
        elif name == "M":
            multiply(h)
        elif name == "W":
            self_copy.wait()
            neigh_copy.wait()
            total = jnp.zeros(acc.shape, F32)
            for g in range(groups):
                total += jnp.dot(mine[g][...].reshape(rows, WIDTHS[g]), self_v[place_of(g)], preferred_element_type=F32)
            acc[...] = total
        elif name == "F":
            last(az, units_a[-1], in_a, h)
            last(by, units_b[-1], in_b, h)
            here = pl.ds(0, WIDTHS[h])
            mean = (summed[:, here] / scale[:, here]).astype(BF16)
            acc[...] += jnp.dot(mean, neigh_v[place_of(h)], preferred_element_type=F32)

    pl.semaphore_wait(barrier, len(hops) + 4)
    start_halo(0)
    row_copy.wait()
    link_slots()
    link_copy.start()
    terms[0] = jnp.zeros_like(terms[0])
    degree_copy.wait()
    for t in range(rows // tile):
        line = jnp.broadcast_to(degree[pl.ds(t, 1), :].astype(F32), (tile, tile))
        for c in range(max(WIDTHS) // tile):
            scale[pl.ds(t * tile, tile), pl.ds(c * tile, tile)] = line.T
    for copy in (link_copy, column_copy, counts_copy, tile_copy):
        copy.wait()
    flying = []
    for item in SCHEDULE:
        run(*item)
        h, name, q, step = item
        if name in "ABZY":
            units_a, units_b, az, by = made[h]
            flying.append(({"A": units_a, "B": units_b, "Z": [az], "Y": [by]}[name][q], step))
        if len(flying) > LAG:
            ring, sent = flying.pop(0)
            ring.drain(sent)
    out[...] = jnp.maximum(acc[...], 0.0).astype(out.dtype)

    for h in range(groups):
        for copy in halo[h]:
            copy.wait_send()
    for ring, sent in flying:
        ring.drain(sent)


def shards(features, tiles, slot_tile_row, slot_tile_column, counts, degree, w_self, w_neigh):
    rows, hidden = features.shape
    slots, tile = tiles.shape[0], tiles.shape[1]
    steps = counts.shape[0]
    ring_y = RING_Y
    ring_z = lax.axis_size("rep") // ring_y
    groups = len(WIDTHS)
    wide = max(WIDTHS)
    rows_b = rows - ROWS_A
    dma = pltpu.SemaphoreType.DMA

    def buffer(*shape):
        return [pltpu.VMEM((2, *shape, width), BF16) for width in WIDTHS]

    n_a, n_b = ring_z // 2 + 1, ring_y // 2 + 1
    last_y, last_z = ring_y // 2, ring_z // 2
    vmem = pl.BlockSpec(memory_space=pltpu.VMEM)
    anywhere = pl.BlockSpec(memory_space=pl.ANY)
    return pl.pallas_call(
        kernel,
        out_shape=jax.ShapeDtypeStruct((rows, hidden), BF16),
        in_specs=[anywhere] * 8,
        out_specs=vmem,
        scratch_shapes=[
            pltpu.VMEM((slots, tile, tile), BF16),
            pltpu.VMEM((slots + 1, tile, wide), F32),
            [pltpu.VMEM((ring_z, ring_y, rows, width), BF16) for width in WIDTHS],
            pltpu.VMEM(w_self.shape, BF16),
            pltpu.VMEM(w_neigh.shape, BF16),
            pltpu.VMEM((rows, wide), F32),
            pltpu.VMEM((rows, hidden), F32),
            pltpu.VMEM((rows, wide), F32),
            buffer(n_a, ROWS_A),
            buffer(ring_z, ROWS_A),
            buffer(ROWS_A),
            buffer(last_z - 1, ROWS_A),
            buffer(n_b, rows_b),
            buffer(last_z - 1, ring_y, rows_b),
            buffer(rows_b),
            buffer(last_y - 1, rows_b),
            *[dma((groups, n_a, 2, last_y))] * 2,
            *[dma((groups, 2, last_z))] * 2,
            *[dma((groups, n_b, 2, last_z))] * 2,
            *[dma((groups, 2, last_y))] * 2,
            dma((groups, steps)),
            dma((groups, steps)),
            dma((8 + groups,)),
            pltpu.VMEM((8, tile), jnp.int32),
            pltpu.SMEM((8, tile), jnp.int32),
            pltpu.VMEM((1, slots), jnp.int32),
            pltpu.SMEM((slots,), jnp.int32),
            pltpu.SMEM((steps,), jnp.int32),
            pltpu.VMEM((rows // tile, tile), jnp.int32),
            [pltpu.VMEM((rows // tile, tile, width), BF16) for width in WIDTHS],
            [[pltpu.VMEM((rows // tile, tile, width), BF16)] * steps for width in WIDTHS],
        ],
        compiler_params=pltpu.CompilerParams(
            collective_id=0, has_side_effects=True, vmem_limit_bytes=56 * 1024 * 1024
        ),
    )(
        slot_tile_row.reshape(1, slots),
        slot_tile_column,
        counts,
        features.reshape(rows // tile, tile, hidden),
        tiles,
        degree.reshape(rows // tile, tile),
        w_self,
        w_neigh,
    )


def solution(mesh):
    return jax.shard_map(
        shards,
        mesh=mesh,
        in_specs=(
            P(("loop", "rep"), None),
            P(("loop", "rep"), None, None),
            P(("loop", "rep")),
            P(("loop", "rep")),
            P(("loop", "rep")),
            P(("loop", "rep")),
            P(),
            P(),
        ),
        out_specs=P(("loop", "rep"), None),
        check_vma=False,
    )
```
